512 devices in a mesh: chan: 4 (over y_hi, core), row: 128 (over x, y_lo, z).
Axes of the slice: x: 4, y: 4 (y_hi: 2, y_lo: 2; y = y_hi * 2 + y_lo), z: 16, core: 2. Of those that a mesh axis runs over, the one named last changes fastest.
Arguments:
- amplitudes: bfloat16 [4, 2048, 256], P('chan', 'row'), may hold values from -6 to 6
- ladder_pp: bfloat16 [4, 2048, 2048], P('chan', 'row'), may hold values from -0.125 to 0.125
- cycle_proton: bfloat16 [4, 2048, 2048], P('chan', 'row'), may hold values from -0.125 to 0.125
- cycle_neutron: bfloat16 [4, 256, 256], P('chan', 'row'), may hold values from -0.375 to 0.375
- recouple: float32 [4, 4], replicated, may hold values from -3 to 3
- proton_live: int32 [4], replicated, may hold values from 2 to 128, as said below
Outputs:
- residual: bfloat16 [4, 2048, 256], P('chan', 'row')
The draws below stay inside these ranges and needn't reach their ends.
Inputs may be any that keep to these rules, and one draw needn't show every extreme that they name: `proton_live`: live proton particle orbitals of each channel; some channel uses all 128.
All inputs are finite; a program needn't handle non-finite values.
Results may differ from the reference program's by a relative error of at most 0.00125.
Values may be sent and summed in bfloat16 or wider, within the bound.
A program may use at most 128 MiB of HBM per device.

```python
import jax
import jax.numpy as jnp
from jax import lax

NA = 128
NB = 16
NI = 16
NJ = 16
NCH = 4
P_SIZE = 2048
HH = 256


def draw_proton_live(key, part):
    key = jax.random.fold_in(key, 7)
    draw_key, pick_key = jax.random.split(key)
    counts = jax.random.randint(draw_key, (NCH,), 2, NA + 1)
    chosen = jax.random.randint(pick_key, (), 0, NCH)
    return jnp.where(jnp.arange(NCH) == chosen, NA, counts).astype(jnp.int32)


def block_scale(stream_key, dims, cuts, least, high):
    loudness, own = 1.0, jax.random.fold_in(stream_key, 6)
    for position, shards_of in cuts:
        steps = jnp.exp(jax.random.uniform(jax.random.fold_in(own, position), (shards_of,), jnp.float32, least / len(cuts), high / len(cuts)))
        loudness = loudness * jnp.repeat(steps, dims[position] // shards_of).reshape([-1 if axis == position else 1 for axis in range(len(dims))])
    return loudness


def scatter_about(own_key, extent, width, bound, pieces=(), kind=jnp.bfloat16):
    result = width * jax.random.normal(own_key, extent, jnp.float32)
    if pieces:
        result = result * block_scale(own_key, extent, pieces, -0.22, 0.18)
    return jnp.clip(result, -bound, bound).astype(kind)


def setup_inputs(seed: int = 0) -> dict:
    keys = jax.random.split(jax.random.key(seed), 7)
    return {
        "amplitudes": scatter_about(keys[0], (NCH, P_SIZE, HH), 1.0, 6.0, ((0, 4), (1, 128))),
        "ladder_pp": scatter_about(keys[1], (NCH, P_SIZE, P_SIZE), P_SIZE ** -0.5, 0.125, ((0, 4), (1, 128))),
        "cycle_proton": scatter_about(keys[2], (NCH, NA * NI, NA * NI), (NA * NI) ** -0.5, 0.125, ((0, 4), (1, 128))),
        "cycle_neutron": scatter_about(keys[3], (NCH, NB * NJ, NB * NJ), (NB * NJ) ** -0.5, 0.375, ((0, 4), (1, 128))),
        "recouple": scatter_about(keys[4], (NCH, NCH), 0.5, 3.0, (), jnp.float32),
        "proton_live": draw_proton_live(jax.random.fold_in(keys[6], 71), 0),
    }


def channel_ladder(operands):
    weights, amplitude = operands
    return jnp.dot(weights, amplitude, preferred_element_type=jnp.float32)


def reference(amplitudes, ladder_pp, cycle_proton, cycle_neutron, recouple, proton_live):
    proton_rows = jnp.arange(NA * NB, dtype=jnp.int32) // NB
    live_mask = proton_rows[None, :] < proton_live[:, None]
    masked = jnp.where(live_mask[:, :, None], amplitudes, jnp.zeros_like(amplitudes))
    ladder = lax.map(channel_ladder, (ladder_pp, masked))
    mixed = jnp.einsum("cd,dph->cph", recouple, masked.astype(jnp.float32), precision=lax.Precision.HIGHEST)
    grid = mixed.reshape(NCH, NA, NB, NI, NJ)
    proton_input = grid.transpose(0, 1, 3, 2, 4).reshape(NCH, NA * NI, NB * NJ)
    proton_term = jnp.einsum("cxy,cyz->cxz", cycle_proton.astype(jnp.float32), proton_input, precision=lax.Precision.HIGHEST)
    proton_term = proton_term.reshape(NCH, NA, NI, NB, NJ).transpose(0, 1, 3, 2, 4).reshape(NCH, NA * NB, NI * NJ)
    neutron_input = grid.transpose(0, 2, 4, 1, 3).reshape(NCH, NB * NJ, NA * NI)
    neutron_term = jnp.einsum("cxy,cyz->cxz", cycle_neutron.astype(jnp.float32), neutron_input, precision=lax.Precision.HIGHEST)
    neutron_term = neutron_term.reshape(NCH, NB, NJ, NA, NI).transpose(0, 3, 1, 4, 2).reshape(NCH, NA * NB, NI * NJ)
    combined = ladder + proton_term + neutron_term
    return jnp.where(live_mask[:, :, None], combined, jnp.float32(0.0)).astype(jnp.bfloat16)
```

```python
import jax
import jax.numpy as jnp
from jax import lax
from jax.experimental import pallas as pl
from jax.experimental.pallas import tpu as pltpu
from jax.sharding import PartitionSpec as P

MESH = pl.DeviceIdType.MESH
F32 = jnp.float32
BF16 = jnp.bfloat16


def swap_rows_lanes(v):
    n, width = v.shape
    lane = lax.broadcasted_iota(jnp.int32, (1, 1, width), 2)
    row = lax.broadcasted_iota(jnp.int32, (1, 8, 1), 1)
    v = v.reshape(n // 8, 8, width)
    for s in range(3):
        step, reach = 1 << s, 8 << s
        lane_bit = (lane & reach) != 0
        row_bit = (row & step) != 0
        down = pltpu.roll(pltpu.roll(v, width - reach, 2), step, 1)
        up = pltpu.roll(pltpu.roll(v, reach, 2), 8 - step, 1)
        moved = jnp.where(row_bit, down, up)
        v = jnp.where(jnp.logical_xor(lane_bit, row_bit), moved, v)
    lane_bit = (lane & 64) != 0
    v = v.reshape(n // 16, 2, 8, width)
    low, high = v[:, 0], v[:, 1]
    new_low = jnp.where(lane_bit, pltpu.roll(high, 64, 2), low)
    new_high = jnp.where(lane_bit, high, pltpu.roll(low, width - 64, 2))
    return jnp.stack([new_low, new_high], axis=1).reshape(n, width)


def lanes_by_half():
    old = lax.broadcasted_iota(jnp.int32, (256, 256), 0)
    new = lax.broadcasted_iota(jnp.int32, (256, 256), 1)
    goes = ((old >> 3) & 1) * 128 + (old >> 4) * 8 + (old & 7)
    return jnp.where(goes == new, 1.0, 0.0).astype(BF16)


def lanes_back():
    new = lax.broadcasted_iota(jnp.int32, (256, 256), 0)
    old = lax.broadcasted_iota(jnp.int32, (256, 256), 1)
    goes = ((old >> 3) & 1) * 128 + (old >> 4) * 8 + (old & 7)
    return jnp.where(goes == new, 1.0, 0.0).astype(BF16)


def neutron_row_order():
    new = lax.broadcasted_iota(jnp.int32, (256, 256), 0)
    old = lax.broadcasted_iota(jnp.int32, (256, 256), 1)
    z, t = old >> 4, old & 1
    b = ((old >> 1) & 7) * 2 + (z >> 3)
    goes = ((z >> 2) & 1) * 128 + b * 8 + (z & 3) * 2 + t
    return jnp.where(goes == new, 1.0, 0.0).astype(BF16)


def mm(a, b):
    return jnp.dot(a, b, preferred_element_type=F32)


def kernel(
    amp, lad, cyc, neu, rec, live, out,
    amp_v, neu_v, zbuf, sall, n1, nall, wl, wc, abuf, fsend, frecv,
    in_sem, own_sem, z_s, z_r, s_s, s_r, n1_s, n1_r, n2_s, n2_r,
    wl_s, wl_r, wc_s, wc_r, a_s, a_r, f_s, f_r,
):
    e, r = lax.axis_index("chan"), lax.axis_index("row")
    yh, co = lax.div(e, 2), lax.rem(e, 2)
    x, yl, z = lax.div(r, 32), lax.rem(lax.div(r, 16), 2), lax.rem(r, 16)
    me = e * 4 + x

    def at_z(k):
        return (e, x * 32 + yl * 16 + lax.rem(z + k + 16, 16))

    def member(k):
        m = lax.rem(me + k, 16)
        return lax.div(m, 4), lax.rem(m, 4)

    def near_z(k):
        return (4 - lax.div(k, 2)) * (1 - 2 * lax.rem(k, 2))

    bar = pltpu.get_barrier_semaphore()

    def greet(dev):
        pl.semaphore_signal(bar, inc=1, device_id=dev, device_id_type=MESH)

    @pl.loop(0, 8)
    def _(k):
        greet(at_z(near_z(k)))

    @pl.loop(1, 16)
    def _(k):
        pe, px = member(k)
        greet((pe, px * 32 + yl * 16 + z))

    @pl.loop(0, 4)
    def _(k):
        greet((k, x * 32 + (1 - yl) * 16 + z))

    @pl.loop(1, 4)
    def _(k):
        greet((e, lax.rem(x + k, 4) * 32 + (1 - yl) * 16 + z))

    get_amp = pltpu.make_async_copy(amp.at[0], amp_v, in_sem.at[0])
    get_neu = pltpu.make_async_copy(neu, neu_v, in_sem.at[1])
    get_amp.start()
    get_neu.start()
    my_rows = pl.ds(pl.multiple_of(me * 16, 16), 16)
    my_cols = pl.ds(pl.multiple_of(x * 512 + yh * 256, 256), 256)
    own_l = pltpu.make_async_copy(lad.at[0, :, my_cols], wl.at[my_rows], own_sem.at[0])
    own_c = pltpu.make_async_copy(cyc.at[0, :, my_cols], wc.at[my_rows], own_sem.at[1])
    own_l.start()
    own_c.start()

    order = lanes_by_half()
    alive = jnp.where(r < live[e], 1.0, 0.0).astype(F32)
    my_z = pl.ds(pl.multiple_of(z * 16, 16), 16)
    my_e = pl.ds(pl.multiple_of(e * 16, 16), 16)
    group = x * 2 + yl
    get_amp.wait()
    block = mm((amp_v[...].astype(F32) * alive).astype(BF16), order)
    zbuf[my_z, :] = block.astype(BF16)
    sall[my_e, :] = swap_rows_lanes(block).astype(BF16)
    get_neu.wait()
    pair = mm(neu_v[0], order)
    place = lax.broadcasted_iota(jnp.int32, (16, 256), 0)
    padded = jnp.where(
        place == 2 * group, pair[0:1], jnp.where(place == 2 * group + 1, pair[1:2], 0.0)
    )
    n1[group] = padded.astype(BF16)

    pl.semaphore_wait(bar, 30)

    def send(src, dst, ss, rs, dev):
        return pltpu.make_async_remote_copy(
            src_ref=src, dst_ref=dst, send_sem=ss, recv_sem=rs,
            device_id=dev, device_id_type=MESH,
        )

    def z_rows(k):
        return pl.ds(pl.multiple_of(lax.rem(z + k + 16, 16) * 16, 16), 16)

    def z_copy(buf, ss, rs, slot, source, to):
        rows = z_rows(source)
        return send(
            buf.at[rows], buf.at[rows], ss.at[slot],
            rs.at[lax.rem(z + source + 16, 16)], at_z(to),
        )

    def z_start(buf, ss, rs):
        @pl.loop(0, 8)
        def _(k):
            z_copy(buf, ss, rs, k, 0, near_z(k)).start()

    def z_wait(buf, ss, rs, source):
        z_copy(buf, ss, rs, 0, source, 1).wait_recv()

    def z_relay(buf, ss, rs):
        z_wait(buf, ss, rs, -4)

        @pl.loop(0, 4)
        def _(k):
            z_copy(buf, ss, rs, 8 + k, -4, 4 - k).start()

        z_wait(buf, ss, rs, 4)

        @pl.loop(0, 3)
        def _(k):
            z_copy(buf, ss, rs, 12 + k, 4, k - 3).start()

    def z_sent(buf, ss, rs):
        @pl.loop(0, 15)
        def _(k):
            z_copy(buf, ss, rs, k, 0, 1).wait_send()

    def n1_copy(k):
        g = lax.rem(group + k, 8)
        dev = (e, lax.div(g, 2) * 32 + lax.rem(g, 2) * 16 + z)
        return send(n1.at[group], n1.at[group], n1_s.at[k], n1_r.at[group], dev)

    def s_copy(k):
        rows = sall.at[my_e]
        return send(rows, rows, s_s.at[k], s_r.at[e], (lax.rem(e + k, 4), r))

    def w_copy(src, dst, ss, rs, k):
        pe, px = member(k)
        cols = pl.ds(pl.multiple_of(px * 512 + lax.div(pe, 2) * 256, 256), 256)
        return send(
            src.at[0, :, cols], dst.at[my_rows], ss.at[k], rs.at[me],
            (pe, px * 32 + yl * 16 + z),
        )

    z_start(zbuf, z_s, z_r)

    @pl.loop(1, 8)
    def _(k):
        n1_copy(k).start()

    @pl.loop(1, 4)
    def _(k):
        s_copy(k).start()

    @pl.loop(1, 16)
    def _(k):
        w_copy(lad, wl, wl_s, wl_r, k).start()
        w_copy(cyc, wc, wc_s, wc_r, k).start()

    z_relay(zbuf, z_s, z_r)

    @pl.loop(1, 8)
    def _(k):
        g = lax.rem(group + k, 8)
        send(n1.at[g], n1.at[g], n1_s.at[k], n1_r.at[g], at_z(1)).wait_recv()

    gathered = n1[0].astype(F32)
    for g in range(1, 8):
        gathered = gathered + n1[g].astype(F32)
    nall[my_z, :] = gathered.astype(BF16)
    z_start(nall, n2_s, n2_r)

    def quarter(t):
        return lax.rem(lax.div(z, 4) + t + 4, 4)

    def a_copy(q, k, t):
        pco, pyl = lax.rem(k, 2), lax.div(k, 2)
        rows = pl.ds(pl.multiple_of(q * 64, 64), 64)
        src = zbuf.at[rows, pl.ds(pl.multiple_of(pco * 128, 128), 128)]
        dst = abuf.at[e, rows]
        return src, dst, a_s.at[t, k], a_r.at[e, q], (yl * 2 + pco, x * 32 + pyl * 16 + z)

    def is_self(k):
        pco, pyl = lax.rem(k, 2), lax.div(k, 2)
        return jnp.logical_and(yh == yl, jnp.logical_and(pco == co, pyl == yl))

    def a_start(t, turn):
        q = quarter(turn)

        @pl.loop(0, 4)
        def _(i):
            away = lax.rem(q * 4 + i - z + 16, 16)
            fresh = jnp.logical_and(away != 0, jnp.logical_and(away != 4, away != 12))

            @pl.when(fresh)
            def _():
                z_wait(zbuf, z_s, z_r, away)

        @pl.loop(0, 4)
        def _(k):
            src, dst, ss, rs, dev = a_copy(q, k, t)
            own = is_self(k)

            @pl.when(own)
            def _():
                pltpu.make_async_copy(src, dst, rs).start()

            @pl.when(jnp.logical_not(own))
            def _():
                send(src, dst, ss, rs, dev).start()

    def a_sent(t):
        @pl.loop(0, 4)
        def _(k):
            src, dst, ss, rs, dev = a_copy(0, k, t)

            @pl.when(jnp.logical_not(is_self(k)))
            def _():
                send(src, dst, ss, rs, dev).wait_send()

    def a_wait(turn):
        q = quarter(turn)
        rows = pl.ds(pl.multiple_of(q * 64, 64), 64)

        @pl.loop(0, 4)
        def _(c):
            dst = abuf.at[c, rows]
            send(dst, dst, a_s.at[0, 0], a_r.at[c, q], at_z(1)).wait_recv()

    a_start(0, 0)
    a_start(1, 1)
    a_start(2, 3)
    z_relay(nall, n2_s, n2_r)
    a_start(3, 2)

    own_l.wait()
    own_c.wait()

    @pl.loop(1, 16)
    def _(k):
        m = lax.rem(me + k, 16)
        rows = pl.ds(pl.multiple_of(m * 16, 16), 16)
        send(wl.at[rows], wl.at[rows], wl_s.at[k], wl_r.at[m], at_z(1)).wait_recv()
        send(wc.at[rows], wc.at[rows], wc_s.at[k], wc_r.at[m], at_z(1)).wait_recv()

    for turn in (0, 1, 3, 2):
        a_wait(turn)

    products = []
    for c in range(4):
        turned = swap_rows_lanes(abuf[c].astype(F32)).astype(BF16)
        products.append(mm(wc[...], turned))
    for c in range(4):
        rows = slice(64 * c, 64 * c + 64)
        mixed = rec[c, 0] * products[0][rows]
        for d in range(1, 4):
            mixed = mixed + rec[c, d] * products[d][rows]
        fsend[rows, :] = swap_rows_lanes(mixed) + mm(wl[rows, :], abuf[c])

    def f_copy(k):
        m = lax.rem(me + k, 16)
        rows = pl.ds(pl.multiple_of(m * 16, 16), 16)
        return send(
            fsend.at[rows], frecv.at[me], f_s.at[k], f_r.at[me],
            (lax.div(m, 4), lax.rem(m, 4) * 32 + yl * 16 + z),
        )

    @pl.loop(1, 16)
    def _(k):
        f_copy(k).start()

    frecv[me] = fsend[my_rows, :]

    @pl.loop(1, 4)
    def _(k):
        c = lax.rem(e + k, 4)
        rows = sall.at[pl.ds(pl.multiple_of(c * 16, 16), 16)]
        send(rows, rows, s_s.at[k], s_r.at[c], at_z(1)).wait_recv()

    @pl.loop(1, 16)
    def _(k):
        @pl.when(jnp.logical_and(k != 4, k != 12))
        def _():
            z_wait(nall, n2_s, n2_r, k)

    sorted_rows = mm(neutron_row_order(), nall[...]).astype(BF16)
    terms = lax.dot_general(
        sall[...], sorted_rows, (((1,), (1,)), ((), ())), preferred_element_type=F32
    )
    neutron = rec[e, 0] * terms[0:16]
    for c in range(1, 4):
        neutron = neutron + rec[e, c] * terms[16 * c : 16 * c + 16]
    neutron = swap_rows_lanes(neutron)
    back = lanes_back()

    @pl.loop(1, 16)
    def _(k):
        m = lax.rem(me + k, 16)
        dst = frecv.at[m]
        send(fsend.at[pl.ds(0, 16)], dst, f_s.at[k], f_r.at[m], at_z(1)).wait_recv()

    halves = []
    for h in range(2):
        total = neutron[:, 128 * h : 128 * h + 128]
        for s in range(2):
            for i in range(4):
                total = total + frecv[(2 * s + h) * 4 + i]
        halves.append((total * alive).astype(BF16))
    result = lax.dot_general(
        jnp.concatenate(halves, axis=1), back, (((1,), (0,)), ((), ())),
        preferred_element_type=F32,
    )
    out[0] = result.astype(BF16)

    z_sent(zbuf, z_s, z_r)
    z_sent(nall, n2_s, n2_r)
    for t in range(4):
        a_sent(t)

    @pl.loop(1, 8)
    def _(k):
        n1_copy(k).wait_send()

    @pl.loop(1, 4)
    def _(k):
        s_copy(k).wait_send()

    @pl.loop(1, 16)
    def _(k):
        w_copy(lad, wl, wl_s, wl_r, k).wait_send()
        w_copy(cyc, wc, wc_s, wc_r, k).wait_send()
        f_copy(k).wait_send()


def local(amplitudes, ladder_pp, cycle_proton, cycle_neutron, recouple, proton_live):
    dma = pltpu.SemaphoreType.DMA
    return pl.pallas_call(
        kernel,
        out_shape=jax.ShapeDtypeStruct((1, 16, 256), BF16),
        in_specs=[pl.BlockSpec(memory_space=pl.ANY)] * 4
        + [pl.BlockSpec(memory_space=pltpu.SMEM)] * 2,
        out_specs=pl.BlockSpec(memory_space=pltpu.VMEM),
        scratch_shapes=[
            pltpu.VMEM((16, 256), BF16),
            pltpu.VMEM((1, 2, 256), BF16),
            pltpu.VMEM((256, 256), BF16),
            pltpu.VMEM((64, 256), BF16),
            pltpu.VMEM((8, 16, 256), BF16),
            pltpu.VMEM((256, 256), BF16),
            pltpu.VMEM((256, 256), BF16),
            pltpu.VMEM((256, 256), BF16),
            pltpu.VMEM((4, 256, 128), BF16),
            pltpu.VMEM((256, 128), F32),
            pltpu.VMEM((16, 16, 128), F32),
            dma((2,)),
            dma((2,)),
            dma((15,)),
            dma((16,)),
            dma((4,)),
            dma((4,)),
            dma((8,)),
            dma((8,)),
            dma((15,)),
            dma((16,)),
            dma((16,)),
            dma((16,)),
            dma((16,)),
            dma((16,)),
            dma((4, 4)),
            dma((4, 4)),
            dma((16,)),
            dma((16,)),
        ],
        compiler_params=pltpu.CompilerParams(
            collective_id=0, has_side_effects=True, vmem_limit_bytes=32 << 20
        ),
        name="pair_residual",
    )(amplitudes, ladder_pp, cycle_proton, cycle_neutron, recouple, proton_live)


def solution(mesh):
    rows = P("chan", "row", None)
    return jax.shard_map(
        local,
        mesh=mesh,
        in_specs=(rows, rows, rows, rows, P(), P()),
        out_specs=rows,
        check_vma=False,
    )
```

```python
import jax
import jax.numpy as jnp
from jax import lax
from jax.experimental import pallas as pl
from jax.experimental.pallas import tpu as pltpu
from jax.sharding import PartitionSpec as P

MESH = pl.DeviceIdType.MESH
F32 = jnp.float32
BF16 = jnp.bfloat16


def swap_rows_lanes(v):
    n, width = v.shape
    lane = lax.broadcasted_iota(jnp.int32, (1, 1, width), 2)
    row = lax.broadcasted_iota(jnp.int32, (1, 8, 1), 1)
    v = v.reshape(n // 8, 8, width)
    for s in range(3):
        step, reach = 1 << s, 8 << s
        lane_bit = (lane & reach) != 0
        row_bit = (row & step) != 0
        down = pltpu.roll(pltpu.roll(v, width - reach, 2), step, 1)
        up = pltpu.roll(pltpu.roll(v, reach, 2), 8 - step, 1)
        moved = jnp.where(row_bit, down, up)
        v = jnp.where(jnp.logical_xor(lane_bit, row_bit), moved, v)
    lane_bit = (lane & 64) != 0
    v = v.reshape(n // 16, 2, 8, width)
    low, high = v[:, 0], v[:, 1]
    new_low = jnp.where(lane_bit, pltpu.roll(high, 64, 2), low)
    new_high = jnp.where(lane_bit, high, pltpu.roll(low, width - 64, 2))
    return jnp.stack([new_low, new_high], axis=1).reshape(n, width)


def lanes_by_half():
    old = lax.broadcasted_iota(jnp.int32, (256, 256), 0)
    new = lax.broadcasted_iota(jnp.int32, (256, 256), 1)
    goes = ((old >> 3) & 1) * 128 + (old >> 4) * 8 + (old & 7)
    return jnp.where(goes == new, 1.0, 0.0).astype(BF16)


def lanes_back():
    new = lax.broadcasted_iota(jnp.int32, (256, 256), 0)
    old = lax.broadcasted_iota(jnp.int32, (256, 256), 1)
    goes = ((old >> 3) & 1) * 128 + (old >> 4) * 8 + (old & 7)
    return jnp.where(goes == new, 1.0, 0.0).astype(BF16)


def neutron_row_order():
    new = lax.broadcasted_iota(jnp.int32, (256, 256), 0)
    old = lax.broadcasted_iota(jnp.int32, (256, 256), 1)
    z, t = (old >> 1) & 15, old & 1
    b = (old >> 5) * 2 + (z >> 3)
    goes = ((z >> 2) & 1) * 128 + b * 8 + (z & 3) * 2 + t
    return jnp.where(goes == new, 1.0, 0.0).astype(BF16)


def mm(a, b):
    return jnp.dot(a, b, preferred_element_type=F32)


NEAR, SLOTS = 9, 16
HERE = 4


def kernel(
    amp, lad, cyc, neu, rec_in, live_in, out,
    rec, live, amp_v, zbuf, nz, sall, nall, wl, wc, abuf, plain, turned, fsend, frecv,
    in_sem, own_sem, z_s, z_r, n_s, n_r, s_s, s_r, n1_s, n1_r,
    wl_s, wl_r, wc_s, wc_r, a_s, a_r, f_s, f_r,
):
    e, r = lax.axis_index("chan"), lax.axis_index("row")
    yh, co = lax.div(e, 2), lax.rem(e, 2)
    x, yl, z = lax.div(r, 32), lax.rem(lax.div(r, 16), 2), lax.rem(r, 16)
    me = e * 4 + x
    group = x * 2 + yl

    get_amp = pltpu.make_async_copy(amp.at[0], amp_v, in_sem.at[0])
    get_live = pltpu.make_async_copy(live_in, live, in_sem.at[1])
    get_rec = pltpu.make_async_copy(rec_in, rec, in_sem.at[2])
    get_neu = pltpu.make_async_copy(neu, nz.at[pl.ds(HERE, 1)], in_sem.at[3])
    my_rows = pl.ds(pl.multiple_of(me * 16, 16), 16)
    my_cols = pl.ds(pl.multiple_of(x * 512 + yh * 256, 256), 256)
    own_l = pltpu.make_async_copy(lad.at[0, :, my_cols], wl.at[my_rows], own_sem.at[0])
    own_c = pltpu.make_async_copy(cyc.at[0, :, my_cols], wc.at[my_rows], own_sem.at[1])
    get_amp.start()
    get_live.start()

    def at_z(k):
        return (e, x * 32 + yl * 16 + lax.rem(z + k + 16, 16))

    def member(k):
        pe = lax.rem(yh + 1 - lax.div(k, 8), 2) * 2 + lax.rem(
            co + 1 - lax.rem(lax.div(k, 4), 2), 2
        )
        px = lax.rem(x + 3 - lax.rem(k, 4), 4)
        return pe, px

    def near_z(k):
        return (4 - lax.div(k, 2)) * (1 - 2 * lax.rem(k, 2))

    bar = pltpu.get_barrier_semaphore()

    def greet(dev):
        pl.semaphore_signal(bar, inc=1, device_id=dev, device_id_type=MESH)

    @pl.loop(0, 8)
    def _(k):
        greet(at_z(near_z(k)))

    @pl.loop(0, 15)
    def _(k):
        pe, px = member(k)
        greet((pe, px * 32 + yl * 16 + z))

    @pl.loop(0, 4)
    def _(k):
        greet((k, x * 32 + (1 - yl) * 16 + z))

    @pl.loop(1, 4)
    def _(k):
        greet((e, lax.rem(x + k, 4) * 32 + (1 - yl) * 16 + z))

    get_neu.start()
    get_rec.start()
    own_l.start()
    own_c.start()

    order = lanes_by_half()
    get_live.wait()
    alive = jnp.where(r < live[e], 1.0, 0.0).astype(F32)
    get_amp.wait()
    block = mm((amp_v[...].astype(F32) * alive).astype(BF16), order)
    zbuf[HERE * 16 : HERE * 16 + 16, :] = block.astype(BF16)
    get_neu.wait()
    get_rec.wait()

    pl.semaphore_wait(bar, 30)

    def send(src, dst, ss, rs, dev):
        return pltpu.make_async_remote_copy(
            src_ref=src, dst_ref=dst, send_sem=ss, recv_sem=rs,
            device_id=dev, device_id_type=MESH,
        )

    def z_rows(slot):
        return pl.ds(pl.multiple_of(slot * 16, 16), 16)

    def z_copy(k, slot, to):
        lands = lax.rem(slot - to + 16, 16)
        return send(
            zbuf.at[z_rows(slot)], zbuf.at[z_rows(lands)], z_s.at[k], z_r.at[lands], at_z(to)
        )

    def n_copy(k, slot, to):
        lands = lax.rem(slot - to + 16, 16)
        return send(
            nz.at[pl.ds(slot, 1)], nz.at[pl.ds(lands, 1)], n_s.at[k], n_r.at[lands], at_z(to)
        )

    def z_wait(slot):
        here = zbuf.at[z_rows(slot)]
        send(here, here, z_s.at[0], z_r.at[slot], at_z(1)).wait_recv()

    def n_wait(slot):
        here = nz.at[pl.ds(slot, 1)]
        send(here, here, n_s.at[0], n_r.at[slot], at_z(1)).wait_recv()

    def relay_low(copy):
        @pl.loop(0, 4)
        def _(k):
            copy(8 + k, 0, 4 - k).start()

    def relay_high(copy):
        @pl.loop(0, 3)
        def _(k):
            copy(12 + k, 8, k - 3).start()

    @pl.loop(0, 8)
    def _(k):
        z_copy(k, HERE, near_z(k)).start()

    def n1_copy(k):
        g = lax.rem(group + k, 8)
        rows = nall.at[pl.ds(pl.multiple_of(group * 32, 32), 32)]
        dev = (e, lax.div(g, 2) * 32 + lax.rem(g, 2) * 16 + z)
        return send(rows, rows, n1_s.at[k], n1_r.at[group], dev)

    my_e = pl.ds(pl.multiple_of(e * 16, 16), 16)

    def s_copy(k):
        rows = sall.at[my_e]
        return send(rows, rows, s_s.at[k], s_r.at[e], (lax.rem(e + k, 4), r))

    def w_copy(src, dst, ss, rs, k):
        pe, px = member(k)
        cols = pl.ds(pl.multiple_of(px * 512 + lax.div(pe, 2) * 256, 256), 256)
        return send(
            src.at[0, :, cols], dst.at[my_rows], ss.at[k], rs.at[me],
            (pe, px * 32 + yl * 16 + z),
        )

    @pl.loop(0, 8)
    def _(k):
        n_copy(k, HERE, near_z(k)).start()

    @pl.loop(0, 15)
    def _(k):
        w_copy(lad, wl, wl_s, wl_r, k).start()
        w_copy(cyc, wc, wc_s, wc_r, k).start()

    sall[my_e, :] = swap_rows_lanes(block).astype(BF16)

    @pl.loop(1, 4)
    def _(k):
        s_copy(k).start()

    z_wait(0)
    relay_low(z_copy)
    z_wait(8)
    relay_high(z_copy)
    n_wait(0)
    relay_low(n_copy)
    n_wait(8)
    relay_high(n_copy)

    def a_copy(part, k):
        pco, pyl = lax.rem(k, 2), lax.div(k, 2)
        rows = pl.ds(0, NEAR * 16) if part == 0 else pl.ds(NEAR * 16, (SLOTS - NEAR) * 16)
        src = zbuf.at[rows, pl.ds(pl.multiple_of(pco * 128, 128), 128)]
        dst = abuf.at[rows, pl.ds(pl.multiple_of(e * 128, 128), 128)]
        dev = (yl * 2 + pco, x * 32 + pyl * 16 + z)
        return src, dst, a_s.at[part, k], a_r.at[part, e], dev

    def is_self(k):
        pco, pyl = lax.rem(k, 2), lax.div(k, 2)
        return jnp.logical_and(yh == yl, jnp.logical_and(pco == co, pyl == yl))

    def a_start(part):
        @pl.loop(0, 4)
        def _(k):
            src, dst, ss, rs, dev = a_copy(part, k)
            own = is_self(k)

            @pl.when(own)
            def _():
                pltpu.make_async_copy(src, dst, rs).start()

            @pl.when(jnp.logical_not(own))
            def _():
                send(src, dst, ss, rs, dev).start()

    def a_sent(part):
        @pl.loop(0, 4)
        def _(k):
            src, dst, ss, rs, dev = a_copy(part, k)

            @pl.when(jnp.logical_not(is_self(k)))
            def _():
                send(src, dst, ss, rs, dev).wait_send()

    def a_wait(part):
        rows = pl.ds(0, NEAR * 16) if part == 0 else pl.ds(NEAR * 16, (SLOTS - NEAR) * 16)

        @pl.loop(0, 4)
        def _(c):
            dst = abuf.at[rows, pl.ds(pl.multiple_of(c * 128, 128), 128)]
            send(dst, dst, a_s.at[0, 0], a_r.at[part, c], at_z(1)).wait_recv()

    def settle(first, last):
        value = abuf[first * 16 : last * 16, :]
        swapped = swap_rows_lanes(value.astype(F32)).astype(BF16)
        for slot in range(first, last):
            rows = pl.ds(pl.multiple_of(lax.rem(z + slot + 12, 16) * 16, 16), 16)
            at = (slot - first) * 16
            plain[rows, :] = value[at : at + 16]
            turned[rows, :] = swapped[at : at + 16]

    @pl.loop(1, 4)
    def _(k):
        z_wait(k)
        z_wait(k + 4)

    a_start(0)

    own_l.wait()
    own_c.wait()

    @pl.loop(0, 15)
    def _(k):
        pe, px = member(k)
        m = pe * 4 + px
        rows = pl.ds(pl.multiple_of(m * 16, 16), 16)
        send(wl.at[rows], wl.at[rows], wl_s.at[k], wl_r.at[m], at_z(1)).wait_recv()
        send(wc.at[rows], wc.at[rows], wc_s.at[k], wc_r.at[m], at_z(1)).wait_recv()

    @pl.loop(NEAR, SLOTS)
    def _(k):
        z_wait(k)

    a_start(1)

    a_wait(0)
    settle(0, NEAR)

    @pl.loop(1, 4)
    def _(k):
        n_wait(k)
        n_wait(k + 4)

    @pl.loop(NEAR, SLOTS)
    def _(k):
        n_wait(k)

    place = lax.broadcasted_iota(jnp.int32, (32, 256), 0)
    stacked = jnp.zeros((32, 256), F32)
    for slot in range(SLOTS):
        at = 2 * lax.rem(z + slot + 12, 16)
        pair = nz[slot].astype(F32)
        stacked = jnp.where(place == at, pair[0:1], stacked)
        stacked = jnp.where(place == at + 1, pair[1:2], stacked)
    nall[pl.ds(pl.multiple_of(group * 32, 32), 32), :] = stacked.astype(BF16)

    @pl.loop(1, 8)
    def _(k):
        n1_copy(k).start()

    a_wait(1)

    settle(NEAR, SLOTS)
    products = mm(wc[...], turned[...])
    for c in range(4):
        rows = slice(64 * c, 64 * c + 64)
        mixed = rec[c, 0] * products[rows, 0:128]
        for d in range(1, 4):
            mixed = mixed + rec[c, d] * products[rows, 128 * d : 128 * d + 128]
        fsend[rows, :] = swap_rows_lanes(mixed) + mm(
            wl[rows, :], plain[:, 128 * c : 128 * c + 128]
        )

    def f_copy(k):
        pe, px = member(k)
        rows = pl.ds(pl.multiple_of((pe * 4 + px) * 16, 16), 16)
        return send(
            fsend.at[rows], frecv.at[me], f_s.at[k], f_r.at[me],
            (pe, px * 32 + yl * 16 + z),
        )

    @pl.loop(0, 15)
    def _(k):
        f_copy(k).start()

    frecv[me] = fsend[my_rows, :]

    @pl.loop(1, 4)
    def _(k):
        c = lax.rem(e + k, 4)
        rows = sall.at[pl.ds(pl.multiple_of(c * 16, 16), 16)]
        send(rows, rows, s_s.at[k], s_r.at[c], at_z(1)).wait_recv()

    @pl.loop(1, 8)
    def _(k):
        g = lax.rem(group + k, 8)
        rows = nall.at[pl.ds(pl.multiple_of(g * 32, 32), 32)]
        send(rows, rows, n1_s.at[k], n1_r.at[g], at_z(1)).wait_recv()

    ordered = mm(neutron_row_order(), nall[...]).astype(BF16)
    ordered = mm(ordered, lanes_by_half()).astype(BF16)
    terms = lax.dot_general(
        sall[...], ordered, (((1,), (1,)), ((), ())), preferred_element_type=F32
    )
    neutron = rec[e, 0] * terms[0:16]
    for c in range(1, 4):
        neutron = neutron + rec[e, c] * terms[16 * c : 16 * c + 16]
    neutron = swap_rows_lanes(neutron)
    back = lanes_back()

    @pl.loop(0, 15)
    def _(k):
        pe, px = member(k)
        m = pe * 4 + px
        send(fsend.at[pl.ds(0, 16)], frecv.at[m], f_s.at[k], f_r.at[m], at_z(1)).wait_recv()

    halves = []
    for h in range(2):
        total = neutron[:, 128 * h : 128 * h + 128]
        for s in range(2):
            for i in range(4):
                total = total + frecv[(2 * s + h) * 4 + i]
        halves.append((total * alive).astype(BF16))
    out[0] = mm(jnp.concatenate(halves, axis=1), back).astype(BF16)

    @pl.loop(0, 8)
    def _(k):
        z_copy(k, HERE, near_z(k)).wait_send()
        n_copy(k, HERE, near_z(k)).wait_send()

    @pl.loop(8, 15)
    def _(k):
        z_copy(k, 0, 1).wait_send()
        n_copy(k, 0, 1).wait_send()

    for part in range(2):
        a_sent(part)

    @pl.loop(1, 8)
    def _(k):
        n1_copy(k).wait_send()

    @pl.loop(1, 4)
    def _(k):
        s_copy(k).wait_send()

    @pl.loop(0, 15)
    def _(k):
        w_copy(lad, wl, wl_s, wl_r, k).wait_send()
        w_copy(cyc, wc, wc_s, wc_r, k).wait_send()
        f_copy(k).wait_send()


def local(amplitudes, ladder_pp, cycle_proton, cycle_neutron, recouple, proton_live):
    dma = pltpu.SemaphoreType.DMA
    operands = (amplitudes, ladder_pp, cycle_proton, cycle_neutron, recouple, proton_live)
    return pl.pallas_call(
        kernel,
        out_shape=pltpu.VMEM((1, 16, 256), BF16),
        in_specs=[pl.BlockSpec(memory_space=pltpu.HBM)] * 6,
        out_specs=pl.BlockSpec(memory_space=pltpu.VMEM),
        scratch_shapes=[
            pltpu.SMEM((4, 4), F32),
            pltpu.SMEM((4,), jnp.int32),
            pltpu.VMEM((16, 256), BF16),
            pltpu.VMEM((256, 256), BF16),
            pltpu.VMEM((16, 2, 256), BF16),
            pltpu.VMEM((64, 256), BF16),
            pltpu.VMEM((256, 256), BF16),
            pltpu.VMEM((256, 256), BF16),
            pltpu.VMEM((256, 256), BF16),
            pltpu.VMEM((256, 512), BF16),
            pltpu.VMEM((256, 512), BF16),
            pltpu.VMEM((256, 512), BF16),
            pltpu.VMEM((256, 128), F32),
            pltpu.VMEM((16, 16, 128), F32),
            dma((4,)),
            dma((2,)),
            dma((15,)),
            dma((16,)),
            dma((15,)),
            dma((16,)),
            dma((4,)),
            dma((4,)),
            dma((8,)),
            dma((8,)),
            dma((15,)),
            dma((16,)),
            dma((15,)),
            dma((16,)),
            dma((2, 4)),
            dma((2, 4)),
            dma((15,)),
            dma((16,)),
        ],
        compiler_params=pltpu.CompilerParams(
            collective_id=0, has_side_effects=True, vmem_limit_bytes=16 << 20
        ),
        name="pair_residual",
    )(*(pltpu.with_memory_space_constraint(v, pltpu.HBM) for v in operands))


def solution(mesh):
    rows = P("chan", "row", None)
    return jax.shard_map(
        local,
        mesh=mesh,
        in_specs=(rows, rows, rows, rows, P(), P()),
        out_specs=rows,
        check_vma=False,
    )
```

```python
import jax
import jax.numpy as jnp
from jax import lax
from jax.experimental import pallas as pl
from jax.experimental.pallas import tpu as pltpu
from jax.sharding import PartitionSpec as P

MESH = pl.DeviceIdType.MESH
F32 = jnp.float32
BF16 = jnp.bfloat16


def swap_rows_lanes(v):
    n, width = v.shape
    lane = lax.broadcasted_iota(jnp.int32, (1, 1, width), 2)
    row = lax.broadcasted_iota(jnp.int32, (1, 8, 1), 1)
    v = v.reshape(n // 8, 8, width)
    for s in range(3):
        step, reach = 1 << s, 8 << s
        lane_bit = (lane & reach) != 0
        row_bit = (row & step) != 0
        down = pltpu.roll(pltpu.roll(v, width - reach, 2), step, 1)
        up = pltpu.roll(pltpu.roll(v, reach, 2), 8 - step, 1)
        moved = jnp.where(row_bit, down, up)
        v = jnp.where(jnp.logical_xor(lane_bit, row_bit), moved, v)
    lane_bit = (lane & 64) != 0
    v = v.reshape(n // 16, 2, 8, width)
    low, high = v[:, 0], v[:, 1]
    new_low = jnp.where(lane_bit, pltpu.roll(high, 64, 2), low)
    new_high = jnp.where(lane_bit, high, pltpu.roll(low, width - 64, 2))
    return jnp.stack([new_low, new_high], axis=1).reshape(n, width)


def lanes_by_half():
    old = lax.broadcasted_iota(jnp.int32, (256, 256), 0)
    new = lax.broadcasted_iota(jnp.int32, (256, 256), 1)
    goes = ((old >> 3) & 1) * 128 + (old >> 4) * 8 + (old & 7)
    return jnp.where(goes == new, 1.0, 0.0).astype(BF16)


def lanes_back():
    new = lax.broadcasted_iota(jnp.int32, (256, 256), 0)
    old = lax.broadcasted_iota(jnp.int32, (256, 256), 1)
    goes = ((old >> 3) & 1) * 128 + (old >> 4) * 8 + (old & 7)
    return jnp.where(goes == new, 1.0, 0.0).astype(BF16)


def neutron_row_order():
    new = lax.broadcasted_iota(jnp.int32, (256, 256), 0)
    old = lax.broadcasted_iota(jnp.int32, (256, 256), 1)
    z, t = (old >> 1) & 15, old & 1
    b = (old >> 5) * 2 + (z >> 3)
    goes = ((z >> 2) & 1) * 128 + b * 8 + (z & 3) * 2 + t
    return jnp.where(goes == new, 1.0, 0.0).astype(BF16)


def div(a, b):
    return a // b if isinstance(a, int) else lax.div(a, b)


def rem(a, b):
    return a % b if isinstance(a, int) else lax.rem(a, b)


def mm(a, b):
    return jnp.dot(a, b, preferred_element_type=F32)


NEAR, SLOTS = 9, 16
LATE, EARLY = 8, 2
HERE = 4


def kernel(
    amp, lad, cyc, neu, rec_in, live_in, out,
    rec, live, amp_v, zbuf, nz, sall, nall, wl, wc, abuf, plain, turned, orders, fsend, frecv,
    in_sem, own_sem, z_s, z_r, n_s, n_r, s_s, s_r, n1_s, n1_r,
    wl_s, wl_r, wc_s, wc_r, a_s, a_r, f_s, f_r,
):
    e, r = lax.axis_index("chan"), lax.axis_index("row")
    yh, co = lax.div(e, 2), lax.rem(e, 2)
    x, yl, z = lax.div(r, 32), lax.rem(lax.div(r, 16), 2), lax.rem(r, 16)
    me = e * 4 + x
    group = x * 2 + yl

    get_amp = pltpu.make_async_copy(amp.at[0], amp_v, in_sem.at[0])
    get_live = pltpu.make_async_copy(live_in, live, in_sem.at[1])
    get_rec = pltpu.make_async_copy(rec_in, rec, in_sem.at[2])
    get_neu = pltpu.make_async_copy(neu, nz.at[pl.ds(HERE, 1)], in_sem.at[3])
    my_rows = pl.ds(pl.multiple_of(me * 16, 16), 16)
    my_cols = pl.ds(pl.multiple_of(x * 512 + co * 256, 256), 256)
    own_l = pltpu.make_async_copy(lad.at[0, :, my_cols], wl.at[my_rows], own_sem.at[0])
    own_c = pltpu.make_async_copy(cyc.at[0, :, my_cols], wc.at[my_rows], own_sem.at[1])
    get_amp.start()
    get_live.start()

    def at_z(k):
        return (e, x * 32 + yl * 16 + lax.rem(z + k + 32, 16))

    def member(k):
        pe = rem(yh + 1 - div(k, 8), 2) * 2 + rem(co + 1 - rem(div(k, 4), 2), 2)
        px = rem(x + 3 - rem(k, 4), 4)
        return pe, px

    def near_z(k):
        return (4 - div(k, 2)) * (1 - 2 * rem(k, 2))

    bar = pltpu.get_barrier_semaphore()

    def greet(dev):
        pl.semaphore_signal(bar, inc=1, device_id=dev, device_id_type=MESH)

    for k in (1, 5, 0, 2, 4, 6, 9, 13):
        pe, px = member(k)
        greet((pe, px * 32 + yl * 16 + z))
        greet(at_z(near_z((1, 5, 0, 2, 4, 6, 9, 13).index(k))))
    for k in (3, 7, 8, 10, 11, 12, 14):
        pe, px = member(k)
        greet((pe, px * 32 + yl * 16 + z))

    def apart(p, q):
        ahead = lax.rem(p - q + 16, 16)
        return jnp.minimum(ahead, 16 - ahead)

    @pl.when(z < EARLY)
    def _():
        @pl.loop(LATE, 16)
        def _(s):
            @pl.when(apart(s, z) > 4)
            def _():
                greet((e, x * 32 + yl * 16 + s))

    for k in range(4):
        greet((k, x * 32 + (1 - yl) * 16 + z))
    for k in range(1, 4):
        greet((e, lax.rem(x + k, 4) * 32 + (1 - yl) * 16 + z))

    get_neu.start()
    get_rec.start()
    own_l.start()
    own_c.start()

    order = lanes_by_half()
    get_live.wait()
    alive = jnp.where(r < live[e], 1.0, 0.0).astype(F32)
    get_amp.wait()
    block = mm((amp_v[...].astype(F32) * alive).astype(BF16), order)
    zbuf[HERE * 16 : HERE * 16 + 16, :] = block.astype(BF16)
    get_neu.wait()
    get_rec.wait()

    straight = 0
    for d in range(EARLY):
        straight = straight + jnp.where(apart(z, d) > 4, 1, 0)
    pl.semaphore_wait(bar, 30 + jnp.where(z >= LATE, straight, 0))

    def send(src, dst, ss, rs, dev):
        return pltpu.make_async_remote_copy(
            src_ref=src, dst_ref=dst, send_sem=ss, recv_sem=rs,
            device_id=dev, device_id_type=MESH,
        )

    def z_rows(slot):
        return pl.ds(pl.multiple_of(slot * 16, 16), 16)

    def z_copy(k, slot, to):
        lands = rem(slot - to + 32, 16)
        return send(
            zbuf.at[z_rows(slot)], zbuf.at[z_rows(lands)], z_s.at[k], z_r.at[lands], at_z(to)
        )

    def n_copy(k, slot, to):
        lands = rem(slot - to + 32, 16)
        return send(
            nz.at[pl.ds(slot, 1)], nz.at[pl.ds(lands, 1)], n_s.at[k], n_r.at[lands], at_z(to)
        )

    def z_wait(slot):
        here = zbuf.at[z_rows(slot)]
        send(here, here, z_s.at[0], z_r.at[slot], at_z(1)).wait_recv()

    def n_wait(slot):
        here = nz.at[pl.ds(slot, 1)]
        send(here, here, n_s.at[0], n_r.at[slot], at_z(1)).wait_recv()

    def goes_straight(source, to):
        return jnp.logical_and(
            lax.rem(z + source + 16, 16) >= LATE, lax.rem(z + to + 16, 16) < EARLY
        )

    def each_straight(act):
        @pl.when(z >= LATE)
        def _():
            @pl.loop(0, EARLY)
            def _(d):
                @pl.when(apart(z, d) > 4)
                def _():
                    act(15 + d, HERE, d - z)

    def each_low(act):
        @pl.loop(0, 4)
        def _(k):
            @pl.when(jnp.logical_not(goes_straight(-4, 4 - k)))
            def _():
                act(8 + k, 0, 4 - k)

    def each_high(act):
        @pl.loop(0, 3)
        def _(k):
            @pl.when(jnp.logical_not(goes_straight(4, k - 3)))
            def _():
                act(12 + k, 8, k - 3)

    def z_start(k, slot, to):
        z_copy(k, slot, to).start()

    def n_start(k, slot, to):
        n_copy(k, slot, to).start()

    def z_sent(k, slot, to):
        z_copy(k, slot, to).wait_send()

    def n_sent(k, slot, to):
        n_copy(k, slot, to).wait_send()

    each_straight(z_start)
    for k in range(8):
        z_copy(k, HERE, near_z(k)).start()

    def n1_copy(k):
        g = lax.rem(group + k, 8)
        rows = nall.at[pl.ds(pl.multiple_of(group * 32, 32), 32)]
        dev = (e, lax.div(g, 2) * 32 + lax.rem(g, 2) * 16 + z)
        return send(rows, rows, n1_s.at[k], n1_r.at[group], dev)

    my_e = pl.ds(pl.multiple_of(e * 16, 16), 16)

    def s_copy(k):
        rows = sall.at[my_e]
        return send(rows, rows, s_s.at[k], s_r.at[e], (lax.rem(e + k, 4), r))

    def w_copy(src, dst, ss, rs, k):
        pe, px = member(k)
        cols = pl.ds(pl.multiple_of(px * 512 + lax.rem(pe, 2) * 256, 256), 256)
        return send(
            src.at[0, :, cols], dst.at[my_rows], ss.at[k], rs.at[me],
            (pe, px * 32 + yl * 16 + z),
        )

    each_straight(n_start)

    @pl.loop(0, 8)
    def _(k):
        n_copy(k, HERE, near_z(k)).start()

    def weights_out():
        @pl.loop(0, 15)
        def _(k):
            w_copy(lad, wl, wl_s, wl_r, k).start()
            w_copy(cyc, wc, wc_s, wc_r, k).start()

    @pl.when(z < LATE)
    def _():
        weights_out()

    z_wait(0)
    each_low(z_start)
    z_wait(8)
    each_high(z_start)
    n_wait(0)
    each_low(n_start)
    n_wait(8)
    each_high(n_start)

    @pl.when(z >= LATE)
    def _():
        weights_out()

    sall[my_e, :] = swap_rows_lanes(block).astype(BF16)

    @pl.loop(1, 4)
    def _(k):
        s_copy(k).start()

    def away_y(k):
        y = lax.rem(yh * 2 + yl + lax.rem(k + 2, 4) + lax.div(k, 2) * (5 - 2 * k), 4)
        return lax.div(y, 2), lax.rem(y, 2)

    def a_copy(part, k):
        pyh, pyl = away_y(k)
        rows = pl.ds(0, NEAR * 16) if part == 0 else pl.ds(NEAR * 16, (SLOTS - NEAR) * 16)
        src = zbuf.at[rows, pl.ds(pl.multiple_of(pyh * 128, 128), 128)]
        dst = abuf.at[rows, pl.ds(pl.multiple_of(e * 128, 128), 128)]
        dev = (pyh * 2 + yl, x * 32 + pyl * 16 + z)
        return src, dst, a_s.at[part, k], a_r.at[part, e], dev

    def is_self(k):
        return jnp.logical_and(co == yl, k == 3)

    def a_start(part):
        @pl.loop(0, 4)
        def _(k):
            src, dst, ss, rs, dev = a_copy(part, k)
            own = is_self(k)

            @pl.when(own)
            def _():
                pltpu.make_async_copy(src, dst, rs).start()

            @pl.when(jnp.logical_not(own))
            def _():
                send(src, dst, ss, rs, dev).start()

    def a_sent(part):
        @pl.loop(0, 4)
        def _(k):
            src, dst, ss, rs, dev = a_copy(part, k)

            @pl.when(jnp.logical_not(is_self(k)))
            def _():
                send(src, dst, ss, rs, dev).wait_send()

    def a_wait(part):
        rows = pl.ds(0, NEAR * 16) if part == 0 else pl.ds(NEAR * 16, (SLOTS - NEAR) * 16)

        @pl.loop(0, 4)
        def _(c):
            dst = abuf.at[rows, pl.ds(pl.multiple_of(c * 128, 128), 128)]
            send(dst, dst, a_s.at[0, 0], a_r.at[part, c], at_z(1)).wait_recv()

    def settle(first, last):
        value = abuf[first * 16 : last * 16, :]
        swapped = swap_rows_lanes(value.astype(F32)).astype(BF16)
        for slot in range(first, last):
            rows = pl.ds(pl.multiple_of(lax.rem(z + slot + 12, 16) * 16, 16), 16)
            at = (slot - first) * 16
            plain[rows, :] = value[at : at + 16]
            turned[rows, :] = swapped[at : at + 16]

    orders[0] = order
    orders[1] = lanes_back()
    orders[2] = neutron_row_order()

    @pl.loop(1, 4)
    def _(k):
        z_wait(k)
        z_wait(k + 4)

    a_start(0)

    own_l.wait()
    own_c.wait()

    @pl.loop(0, 15)
    def _(k):
        pe, px = member(k)
        m = pe * 4 + px
        rows = pl.ds(pl.multiple_of(m * 16, 16), 16)
        send(wl.at[rows], wl.at[rows], wl_s.at[k], wl_r.at[m], at_z(1)).wait_recv()
        send(wc.at[rows], wc.at[rows], wc_s.at[k], wc_r.at[m], at_z(1)).wait_recv()

    @pl.loop(NEAR, SLOTS)
    def _(k):
        z_wait(k)

    a_start(1)

    @pl.loop(1, 4)
    def _(k):
        n_wait(k)
        n_wait(k + 4)

    @pl.loop(NEAR, SLOTS)
    def _(k):
        n_wait(k)

    place = lax.broadcasted_iota(jnp.int32, (32, 256), 0)
    stacked = jnp.zeros((32, 256), F32)
    for slot in range(SLOTS):
        at = 2 * lax.rem(z + slot + 12, 16)
        pair = nz[slot].astype(F32)
        stacked = jnp.where(place == at, pair[0:1], stacked)
        stacked = jnp.where(place == at + 1, pair[1:2], stacked)
    nall[pl.ds(pl.multiple_of(group * 32, 32), 32), :] = stacked.astype(BF16)

    @pl.loop(1, 8)
    def _(k):
        n1_copy(k).start()

    a_wait(0)
    settle(0, NEAR)

    a_wait(1)

    settle(NEAR, SLOTS)
    products = mm(wc[...], turned[...])
    for c in range(4):
        rows = slice(64 * c, 64 * c + 64)
        mixed = rec[c, 0] * products[rows, 0:128]
        for d in range(1, 4):
            mixed = mixed + rec[c, d] * products[rows, 128 * d : 128 * d + 128]
        fsend[rows, :] = swap_rows_lanes(mixed) + mm(
            wl[rows, :], plain[:, 128 * c : 128 * c + 128]
        )

    def f_copy(k):
        pe, px = member(k)
        rows = pl.ds(pl.multiple_of((pe * 4 + px) * 16, 16), 16)
        return send(
            fsend.at[rows], frecv.at[me], f_s.at[k], f_r.at[me],
            (pe, px * 32 + yl * 16 + z),
        )

    for k in (1, 5, 0, 2, 4, 6, 9, 13, 3, 7, 8, 10, 11, 12, 14):
        f_copy(k).start()

    frecv[me] = fsend[my_rows, :]

    @pl.loop(1, 4)
    def _(k):
        c = lax.rem(e + k, 4)
        rows = sall.at[pl.ds(pl.multiple_of(c * 16, 16), 16)]
        send(rows, rows, s_s.at[k], s_r.at[c], at_z(1)).wait_recv()

    @pl.loop(1, 8)
    def _(k):
        g = lax.rem(group + k, 8)
        rows = nall.at[pl.ds(pl.multiple_of(g * 32, 32), 32)]
        send(rows, rows, n1_s.at[k], n1_r.at[g], at_z(1)).wait_recv()

    ordered = mm(orders[2], nall[...]).astype(BF16)
    ordered = mm(ordered, orders[0]).astype(BF16)
    terms = lax.dot_general(
        sall[...], ordered, (((1,), (1,)), ((), ())), preferred_element_type=F32
    )
    neutron = rec[e, 0] * terms[0:16]
    for c in range(1, 4):
        neutron = neutron + rec[e, c] * terms[16 * c : 16 * c + 16]
    neutron = swap_rows_lanes(neutron)

    @pl.loop(0, 8)
    def _(k):
        z_copy(k, HERE, near_z(k)).wait_send()
        n_copy(k, HERE, near_z(k)).wait_send()

    for sent in (z_sent, n_sent):
        each_straight(sent)
        each_low(sent)
        each_high(sent)

    for part in range(2):
        a_sent(part)

    @pl.loop(1, 8)
    def _(k):
        n1_copy(k).wait_send()

    @pl.loop(1, 4)
    def _(k):
        s_copy(k).wait_send()

    @pl.loop(0, 15)
    def _(k):
        w_copy(lad, wl, wl_s, wl_r, k).wait_send()
        w_copy(cyc, wc, wc_s, wc_r, k).wait_send()
        f_copy(k).wait_send()

    @pl.loop(0, 15)
    def _(k):
        pe, px = member(k)
        m = pe * 4 + px
        send(fsend.at[pl.ds(0, 16)], frecv.at[m], f_s.at[k], f_r.at[m], at_z(1)).wait_recv()

    halves = []
    for h in range(2):
        total = neutron[:, 128 * h : 128 * h + 128]
        for s in range(2):
            for i in range(4):
                total = total + frecv[(2 * h + s) * 4 + i]
        halves.append((total * alive).astype(BF16))
    out[0] = mm(jnp.concatenate(halves, axis=1), orders[1]).astype(BF16)


def local(amplitudes, ladder_pp, cycle_proton, cycle_neutron, recouple, proton_live):
    dma = pltpu.SemaphoreType.DMA
    operands = (amplitudes, ladder_pp, cycle_proton, cycle_neutron, recouple, proton_live)
    return pl.pallas_call(
        kernel,
        out_shape=pltpu.VMEM((1, 16, 256), BF16),
        in_specs=[pl.BlockSpec(memory_space=pltpu.HBM)] * 6,
        out_specs=pl.BlockSpec(memory_space=pltpu.VMEM),
        scratch_shapes=[
            pltpu.SMEM((4, 4), F32),
            pltpu.SMEM((4,), jnp.int32),
            pltpu.VMEM((16, 256), BF16),
            pltpu.VMEM((256, 256), BF16),
            pltpu.VMEM((16, 2, 256), BF16),
            pltpu.VMEM((64, 256), BF16),
            pltpu.VMEM((256, 256), BF16),
            pltpu.VMEM((256, 256), BF16),
            pltpu.VMEM((256, 256), BF16),
            pltpu.VMEM((256, 512), BF16),
            pltpu.VMEM((256, 512), BF16),
            pltpu.VMEM((256, 512), BF16),
            pltpu.VMEM((3, 256, 256), BF16),
            pltpu.VMEM((256, 128), F32),
            pltpu.VMEM((16, 16, 128), F32),
            dma((4,)),
            dma((2,)),
            dma((15 + EARLY,)),
            dma((16,)),
            dma((15 + EARLY,)),
            dma((16,)),
            dma((4,)),
            dma((4,)),
            dma((8,)),
            dma((8,)),
            dma((15,)),
            dma((16,)),
            dma((15,)),
            dma((16,)),
            dma((2, 4)),
            dma((2, 4)),
            dma((15,)),
            dma((16,)),
        ],
        compiler_params=pltpu.CompilerParams(
            collective_id=0, has_side_effects=True, vmem_limit_bytes=16 << 20
        ),
        name="pair_residual",
    )(*(pltpu.with_memory_space_constraint(v, pltpu.HBM) for v in operands))


def solution(mesh):
    rows = P("chan", "row", None)
    return jax.shard_map(
        local,
        mesh=mesh,
        in_specs=(rows, rows, rows, rows, P(), P()),
        out_specs=rows,
        check_vma=False,
    )
```

```python
import jax
import jax.numpy as jnp
from jax import lax
from jax.experimental import pallas as pl
from jax.experimental.pallas import tpu as pltpu
from jax.sharding import PartitionSpec as P

MESH = pl.DeviceIdType.MESH
F32 = jnp.float32
BF16 = jnp.bfloat16


def swap_rows_lanes(v):
    n, width = v.shape
    lane = lax.broadcasted_iota(jnp.int32, (1, 1, width), 2)
    row = lax.broadcasted_iota(jnp.int32, (1, 8, 1), 1)
    v = v.reshape(n // 8, 8, width)
    for s in range(3):
        step, reach = 1 << s, 8 << s
        lane_bit = (lane & reach) != 0
        row_bit = (row & step) != 0
        down = pltpu.roll(pltpu.roll(v, width - reach, 2), step, 1)
        up = pltpu.roll(pltpu.roll(v, reach, 2), 8 - step, 1)
        moved = jnp.where(row_bit, down, up)
        v = jnp.where(jnp.logical_xor(lane_bit, row_bit), moved, v)
    lane_bit = (lane & 64) != 0
    v = v.reshape(n // 16, 2, 8, width)
    low, high = v[:, 0], v[:, 1]
    new_low = jnp.where(lane_bit, pltpu.roll(high, 64, 2), low)
    new_high = jnp.where(lane_bit, high, pltpu.roll(low, width - 64, 2))
    return jnp.stack([new_low, new_high], axis=1).reshape(n, width)


def lanes_by_half():
    old = lax.broadcasted_iota(jnp.int32, (256, 256), 0)
    new = lax.broadcasted_iota(jnp.int32, (256, 256), 1)
    goes = ((old >> 3) & 1) * 128 + (old >> 4) * 8 + (old & 7)
    return jnp.where(goes == new, 1.0, 0.0).astype(BF16)


def lanes_back():
    new = lax.broadcasted_iota(jnp.int32, (256, 256), 0)
    old = lax.broadcasted_iota(jnp.int32, (256, 256), 1)
    goes = ((old >> 3) & 1) * 128 + (old >> 4) * 8 + (old & 7)
    return jnp.where(goes == new, 1.0, 0.0).astype(BF16)


def neutron_row_order():
    new = lax.broadcasted_iota(jnp.int32, (256, 256), 0)
    old = lax.broadcasted_iota(jnp.int32, (256, 256), 1)
    z, t = (old >> 1) & 15, old & 1
    b = (old >> 5) * 2 + (z >> 3)
    goes = ((z >> 2) & 1) * 128 + b * 8 + (z & 3) * 2 + t
    return jnp.where(goes == new, 1.0, 0.0).astype(BF16)


def div(a, b):
    return a // b if isinstance(a, int) else lax.div(a, b)


def rem(a, b):
    return a % b if isinstance(a, int) else lax.rem(a, b)


def mm(a, b):
    return jnp.dot(a, b, preferred_element_type=F32)


SLOTS = 16
PARTS = ((4, 9), (0, 4), (9, 12), (12, 16))
LATE, EARLY = 8, 2
HERE = 4


def kernel(
    amp, lad, cyc, neu, rec_in, live_in, out,
    rec, live, amp_v, zbuf, nz, sall, nall, wts, abuf, plain, turned, orders, fsend, frecv,
    in_sem, z_s, z_r, n_s, n_r, s_s, s_r, n1_s, n1_r,
    w_s, w_r, a_s, a_r, f_s, f_r,
):
    e, r = lax.axis_index("chan"), lax.axis_index("row")
    yh, co = lax.div(e, 2), lax.rem(e, 2)
    x, yl, z = lax.div(r, 32), lax.rem(lax.div(r, 16), 2), lax.rem(r, 16)
    me = e * 4 + x
    group = x * 2 + yl

    get_amp = pltpu.make_async_copy(amp.at[0], amp_v, in_sem.at[0])
    get_live = pltpu.make_async_copy(live_in, live, in_sem.at[1])
    get_rec = pltpu.make_async_copy(rec_in, rec, in_sem.at[2])
    get_neu = pltpu.make_async_copy(neu, nz.at[pl.ds(HERE, 1)], in_sem.at[3])
    my_rows = pl.ds(pl.multiple_of(me * 16, 16), 16)
    low_rows = pl.ds(pl.multiple_of(256 + me * 16, 16), 16)
    my_cols = pl.ds(pl.multiple_of(x * 512 + co * 256, 256), 256)
    own_l = pltpu.make_async_copy(lad.at[0, :, my_cols], wts.at[my_rows], w_r)
    own_c = pltpu.make_async_copy(cyc.at[0, :, my_cols], wts.at[low_rows], w_r)
    get_amp.start()
    get_live.start()

    def at_z(k):
        return (e, x * 32 + yl * 16 + lax.rem(z + k + 32, 16))

    def member(k):
        pe = rem(yh + 1 - div(k, 8), 2) * 2 + rem(co + 1 - rem(div(k, 4), 2), 2)
        px = rem(x + 3 - rem(k, 4), 4)
        return pe, px

    def near_z(k):
        return (4 - div(k, 2)) * (1 - 2 * rem(k, 2))

    bar = pltpu.get_barrier_semaphore()

    def greet(dev):
        pl.semaphore_signal(bar, inc=1, device_id=dev, device_id_type=MESH)

    for k in (1, 5, 0, 2, 4, 6, 9, 13):
        pe, px = member(k)
        greet((pe, px * 32 + yl * 16 + z))
        greet(at_z(near_z((1, 5, 0, 2, 4, 6, 9, 13).index(k))))
    for k in (3, 7, 8, 10, 11, 12, 14):
        pe, px = member(k)
        greet((pe, px * 32 + yl * 16 + z))

    def apart(p, q):
        ahead = lax.rem(p - q + 16, 16)
        return jnp.minimum(ahead, 16 - ahead)

    @pl.when(z < EARLY)
    def _():
        @pl.loop(LATE, 16)
        def _(s):
            @pl.when(apart(s, z) > 4)
            def _():
                greet((e, x * 32 + yl * 16 + s))

    for k in range(4):
        greet((k, x * 32 + (1 - yl) * 16 + z))
    for k in range(1, 4):
        greet((e, lax.rem(x + k, 4) * 32 + (1 - yl) * 16 + z))

    get_neu.start()
    get_rec.start()
    own_l.start()
    own_c.start()

    order = lanes_by_half()
    get_live.wait()
    alive = jnp.where(r < live[e], 1.0, 0.0).astype(F32)
    get_amp.wait()
    block = mm((amp_v[...].astype(F32) * alive).astype(BF16), order)
    zbuf[HERE * 16 : HERE * 16 + 16, :] = block.astype(BF16)

    straight = 0
    for d in range(EARLY):
        straight = straight + jnp.where(apart(z, d) > 4, 1, 0)
    pl.semaphore_wait(bar, 30 + jnp.where(z >= LATE, straight, 0))

    def send(src, dst, ss, rs, dev):
        return pltpu.make_async_remote_copy(
            src_ref=src, dst_ref=dst, send_sem=ss, recv_sem=rs,
            device_id=dev, device_id_type=MESH,
        )

    def z_rows(slot):
        return pl.ds(pl.multiple_of(slot * 16, 16), 16)

    def z_copy(k, slot, to):
        lands = rem(slot - to + 32, 16)
        return send(
            zbuf.at[z_rows(slot)], zbuf.at[z_rows(lands)], z_s.at[k], z_r.at[lands], at_z(to)
        )

    def n_copy(k, slot, to):
        lands = rem(slot - to + 32, 16)
        return send(
            nz.at[pl.ds(slot, 1)], nz.at[pl.ds(lands, 1)], n_s.at[k], n_r.at[lands], at_z(to)
        )

    def z_wait(slot):
        here = zbuf.at[z_rows(slot)]
        send(here, here, z_s.at[0], z_r.at[slot], at_z(1)).wait_recv()

    def n_wait(slot):
        here = nz.at[pl.ds(slot, 1)]
        send(here, here, n_s.at[0], n_r.at[slot], at_z(1)).wait_recv()

    def goes_straight(source, to):
        return jnp.logical_and(
            lax.rem(z + source + 16, 16) >= LATE, lax.rem(z + to + 16, 16) < EARLY
        )

    def each_straight(act):
        @pl.when(z >= LATE)
        def _():
            @pl.loop(0, EARLY)
            def _(d):
                @pl.when(apart(z, d) > 4)
                def _():
                    act(15 + d, HERE, d - z)

    def each_low(act):
        @pl.loop(0, 4)
        def _(k):
            @pl.when(jnp.logical_not(goes_straight(-4, 4 - k)))
            def _():
                act(8 + k, 0, 4 - k)

    def each_high(act):
        @pl.loop(0, 3)
        def _(k):
            @pl.when(jnp.logical_not(goes_straight(4, k - 3)))
            def _():
                act(12 + k, 8, k - 3)

    def z_start(k, slot, to):
        z_copy(k, slot, to).start()

    def n_start(k, slot, to):
        n_copy(k, slot, to).start()

    def z_sent(k, slot, to):
        z_copy(k, slot, to).wait_send()

    def n_sent(k, slot, to):
        n_copy(k, slot, to).wait_send()

    each_straight(z_start)
    for k in range(8):
        z_copy(k, HERE, near_z(k)).start()

    def n1_copy(k):
        g = lax.rem(group + k, 8)
        rows = nall.at[pl.ds(pl.multiple_of(group * 32, 32), 32)]
        dev = (e, lax.div(g, 2) * 32 + lax.rem(g, 2) * 16 + z)
        return send(rows, rows, n1_s, n1_r, dev)

    my_e = pl.ds(pl.multiple_of(e * 16, 16), 16)

    def s_copy(k):
        rows = sall.at[my_e]
        return send(rows, rows, s_s, s_r, (lax.rem(e + k, 4), r))

    def w_copy(src, rows, k):
        pe, px = member(k)
        cols = pl.ds(pl.multiple_of(px * 512 + lax.rem(pe, 2) * 256, 256), 256)
        return send(
            src.at[0, :, cols], wts.at[rows], w_s, w_r, (pe, px * 32 + yl * 16 + z)
        )

    def all_here(ref, sem):
        send(ref, ref, sem, sem, at_z(1)).wait_recv()

    def all_gone(ref, sem):
        send(ref, ref, sem, sem, at_z(1)).wait_send()

    get_neu.wait()
    get_rec.wait()
    each_straight(n_start)

    @pl.loop(0, 8)
    def _(k):
        n_copy(k, HERE, near_z(k)).start()

    def weights_out():
        @pl.loop(0, 15)
        def _(k):
            w_copy(lad, my_rows, k).start()
            w_copy(cyc, low_rows, k).start()

    @pl.when(z < LATE)
    def _():
        weights_out()

    def away_y(k):
        y = lax.rem(yh * 2 + yl + lax.rem(k + 2, 4) + lax.div(k, 2) * (5 - 2 * k), 4)
        return lax.div(y, 2), lax.rem(y, 2)

    def part_rows(part):
        first, last = PARTS[part]
        return pl.ds(first * 16, (last - first) * 16)

    def a_copy(part, k):
        pyh, pyl = away_y(k)
        rows = part_rows(part)
        src = zbuf.at[rows, pl.ds(pl.multiple_of(pyh * 128, 128), 128)]
        dst = abuf.at[rows, pl.ds(pl.multiple_of(e * 128, 128), 128)]
        dev = (pyh * 2 + yl, x * 32 + pyl * 16 + z)
        return src, dst, a_s.at[part, k], a_r.at[part, e], dev

    def is_self(k):
        return jnp.logical_and(co == yl, k == 3)

    def a_start(part):
        @pl.loop(0, 4)
        def _(k):
            src, dst, ss, rs, dev = a_copy(part, k)
            own = is_self(k)

            @pl.when(own)
            def _():
                pltpu.make_async_copy(src, dst, rs).start()

            @pl.when(jnp.logical_not(own))
            def _():
                send(src, dst, ss, rs, dev).start()

    def a_sent(part):
        @pl.loop(0, 4)
        def _(k):
            src, dst, ss, rs, dev = a_copy(part, k)

            @pl.when(jnp.logical_not(is_self(k)))
            def _():
                send(src, dst, ss, rs, dev).wait_send()

    def a_wait(part):
        rows = part_rows(part)

        @pl.loop(0, 4)
        def _(c):
            dst = abuf.at[rows, pl.ds(pl.multiple_of(c * 128, 128), 128)]
            send(dst, dst, a_s.at[0, 0], a_r.at[part, c], at_z(1)).wait_recv()

    for slot in (5, 6, 7, 8):
        z_wait(slot)
    each_high(z_start)
    a_start(0)
    z_wait(0)
    each_low(z_start)
    for slot in (1, 2, 3):
        z_wait(slot)
    a_start(1)
    n_wait(0)
    each_low(n_start)
    n_wait(8)
    each_high(n_start)

    @pl.when(z >= LATE)
    def _():
        weights_out()

    sall[my_e, :] = swap_rows_lanes(block).astype(BF16)

    @pl.loop(1, 4)
    def _(k):
        s_copy(k).start()

    def settle(first, last):
        value = abuf[first * 16 : last * 16, :]
        swapped = swap_rows_lanes(value.astype(F32)).astype(BF16)
        for slot in range(first, last):
            rows = pl.ds(pl.multiple_of(lax.rem(z + slot + 12, 16) * 16, 16), 16)
            at = (slot - first) * 16
            plain[rows, :] = value[at : at + 16]
            turned[rows, :] = swapped[at : at + 16]

    orders[0] = order
    orders[1] = lanes_back()
    orders[2] = neutron_row_order()

    all_here(wts, w_r)

    all_gone(sall.at[0:48], s_s)
    all_gone(wts.at[0:480], w_s)

    @pl.loop(0, 8)
    def _(k):
        z_copy(k, HERE, near_z(k)).wait_send()
        n_copy(k, HERE, near_z(k)).wait_send()

    for part in (2, 3):
        for slot in range(*PARTS[part]):
            z_wait(slot)
        a_start(part)

    a_wait(0)
    a_wait(1)
    settle(0, 9)

    @pl.loop(1, 4)
    def _(k):
        n_wait(k)
        n_wait(k + 4)

    @pl.loop(9, SLOTS)
    def _(k):
        n_wait(k)

    place = lax.broadcasted_iota(jnp.int32, (32, 256), 0)
    stacked = jnp.zeros((32, 256), F32)
    for slot in range(SLOTS):
        at = 2 * lax.rem(z + slot + 12, 16)
        pair = nz[slot].astype(F32)
        stacked = jnp.where(place == at, pair[0:1], stacked)
        stacked = jnp.where(place == at + 1, pair[1:2], stacked)
    nall[pl.ds(pl.multiple_of(group * 32, 32), 32), :] = stacked.astype(BF16)

    @pl.loop(1, 8)
    def _(k):
        n1_copy(k).start()

    for sent in (z_sent, n_sent):
        each_straight(sent)
        each_low(sent)
        each_high(sent)

    a_wait(2)
    settle(9, 12)
    a_wait(3)

    settle(12, 16)
    products = mm(wts[256:512, :], turned[...])
    for c in range(4):
        rows = slice(64 * c, 64 * c + 64)
        mixed = rec[c, 0] * products[rows, 0:128]
        for d in range(1, 4):
            mixed = mixed + rec[c, d] * products[rows, 128 * d : 128 * d + 128]
        fsend[rows, :] = swap_rows_lanes(mixed) + mm(
            wts[rows, :], plain[:, 128 * c : 128 * c + 128]
        )

    def f_copy(k):
        pe, px = member(k)
        rows = pl.ds(pl.multiple_of((pe * 4 + px) * 16, 16), 16)
        return send(
            fsend.at[rows], frecv.at[me], f_s, f_r,
            (pe, px * 32 + yl * 16 + z),
        )

    for k in (1, 5, 0, 2, 4, 6, 9, 13, 3, 7, 8, 10, 11, 12, 14):
        f_copy(k).start()

    frecv[me] = fsend[my_rows, :]

    all_here(sall.at[0:48], s_r)
    all_here(nall.at[0:224], n1_r)

    ordered = mm(orders[2], nall[...]).astype(BF16)
    ordered = mm(ordered, orders[0]).astype(BF16)
    terms = lax.dot_general(
        sall[...], ordered, (((1,), (1,)), ((), ())), preferred_element_type=F32
    )
    neutron = rec[e, 0] * terms[0:16]
    for c in range(1, 4):
        neutron = neutron + rec[e, c] * terms[16 * c : 16 * c + 16]
    neutron = swap_rows_lanes(neutron)

    for part in range(4):
        a_sent(part)

    all_gone(nall.at[0:224], n1_s)
    all_gone(fsend.at[0:240], f_s)

    all_here(frecv.at[0:15], f_r)

    halves = []
    for h in range(2):
        total = neutron[:, 128 * h : 128 * h + 128]
        for s in range(2):
            for i in range(4):
                total = total + frecv[(2 * h + s) * 4 + i]
        halves.append((total * alive).astype(BF16))
    out[0] = mm(jnp.concatenate(halves, axis=1), orders[1]).astype(BF16)


def local(amplitudes, ladder_pp, cycle_proton, cycle_neutron, recouple, proton_live):
    dma = pltpu.SemaphoreType.DMA
    operands = (amplitudes, ladder_pp, cycle_proton, cycle_neutron, recouple, proton_live)
    return pl.pallas_call(
        kernel,
        out_shape=pltpu.VMEM((1, 16, 256), BF16),
        in_specs=[pl.BlockSpec(memory_space=pltpu.HBM)] * 6,
        out_specs=pl.BlockSpec(memory_space=pltpu.VMEM),
        scratch_shapes=[
            pltpu.SMEM((4, 4), F32),
            pltpu.SMEM((4,), jnp.int32),
            pltpu.VMEM((16, 256), BF16),
            pltpu.VMEM((256, 256), BF16),
            pltpu.VMEM((16, 2, 256), BF16),
            pltpu.VMEM((64, 256), BF16),
            pltpu.VMEM((256, 256), BF16),
            pltpu.VMEM((512, 256), BF16),
            pltpu.VMEM((256, 512), BF16),
            pltpu.VMEM((256, 512), BF16),
            pltpu.VMEM((256, 512), BF16),
            pltpu.VMEM((3, 256, 256), BF16),
            pltpu.VMEM((256, 128), F32),
            pltpu.VMEM((16, 16, 128), F32),
            dma((4,)),
            dma((15 + EARLY,)),
            dma((16,)),
            dma((15 + EARLY,)),
            dma((16,)),
            dma,
            dma,
            dma,
            dma,
            dma,
            dma,
            dma((4, 4)),
            dma((4, 4)),
            dma,
            dma,
        ],
        compiler_params=pltpu.CompilerParams(
            collective_id=0, has_side_effects=True, vmem_limit_bytes=16 << 20
        ),
        name="pair_residual",
    )(*(pltpu.with_memory_space_constraint(v, pltpu.HBM) for v in operands))


def solution(mesh):
    rows = P("chan", "row", None)
    return jax.shard_map(
        local,
        mesh=mesh,
        in_specs=(rows, rows, rows, rows, P(), P()),
        out_specs=rows,
        check_vma=False,
    )
```

```python
import jax
import jax.numpy as jnp
from jax import lax
from jax.experimental import pallas as pl
from jax.experimental.pallas import tpu as pltpu
from jax.sharding import PartitionSpec as P

MESH = pl.DeviceIdType.MESH
F32 = jnp.float32
BF16 = jnp.bfloat16


def swap_rows_lanes(v):
    n, width = v.shape
    lane = lax.broadcasted_iota(jnp.int32, (1, 1, width), 2)
    row = lax.broadcasted_iota(jnp.int32, (1, 8, 1), 1)
    v = v.reshape(n // 8, 8, width)
    for s in range(3):
        step, reach = 1 << s, 8 << s
        lane_bit = (lane & reach) != 0
        row_bit = (row & step) != 0
        down = pltpu.roll(pltpu.roll(v, width - reach, 2), step, 1)
        up = pltpu.roll(pltpu.roll(v, reach, 2), 8 - step, 1)
        moved = jnp.where(row_bit, down, up)
        v = jnp.where(jnp.logical_xor(lane_bit, row_bit), moved, v)
    lane_bit = (lane & 64) != 0
    v = v.reshape(n // 16, 2, 8, width)
    low, high = v[:, 0], v[:, 1]
    new_low = jnp.where(lane_bit, pltpu.roll(high, 64, 2), low)
    new_high = jnp.where(lane_bit, high, pltpu.roll(low, width - 64, 2))
    return jnp.stack([new_low, new_high], axis=1).reshape(n, width)


def lanes_by_half():
    old = lax.broadcasted_iota(jnp.int32, (256, 256), 0)
    new = lax.broadcasted_iota(jnp.int32, (256, 256), 1)
    goes = ((old >> 3) & 1) * 128 + (old >> 4) * 8 + (old & 7)
    return jnp.where(goes == new, 1.0, 0.0).astype(BF16)


def lanes_back():
    new = lax.broadcasted_iota(jnp.int32, (256, 256), 0)
    old = lax.broadcasted_iota(jnp.int32, (256, 256), 1)
    goes = ((old >> 3) & 1) * 128 + (old >> 4) * 8 + (old & 7)
    return jnp.where(goes == new, 1.0, 0.0).astype(BF16)


def neutron_row_order():
    new = lax.broadcasted_iota(jnp.int32, (256, 256), 0)
    old = lax.broadcasted_iota(jnp.int32, (256, 256), 1)
    z, t = (old >> 1) & 15, old & 1
    b = (old >> 5) * 2 + (z >> 3)
    goes = ((z >> 2) & 1) * 128 + b * 8 + (z & 3) * 2 + t
    return jnp.where(goes == new, 1.0, 0.0).astype(BF16)


def div(a, b):
    return a // b if isinstance(a, int) else lax.div(a, b)


def rem(a, b):
    return a % b if isinstance(a, int) else lax.rem(a, b)


def mm(a, b):
    return jnp.dot(a, b, preferred_element_type=F32)


SLOTS = 16
PARTS = ((4, 9), (0, 4), (9, 13), (13, 16))
LATE, EARLY = 8, 2
HERE = 4


def kernel(
    amp, lad, cyc, neu, rec_in, live_in, out,
    rec, live, amp_v, zbuf, nz, sall, nall, wts, abuf, plain, turned, orders, fsend, frecv,
    in_sem, z_s, z_r, n_s, n_r, s_s, s_r, n1_s, n1_r,
    w_s, w_r, a_s, a_r, f_s, f_r,
):
    e, r = lax.axis_index("chan"), lax.axis_index("row")
    yh, co = lax.div(e, 2), lax.rem(e, 2)
    x, yl, z = lax.div(r, 32), lax.rem(lax.div(r, 16), 2), lax.rem(r, 16)
    me = e * 4 + x
    group = x * 2 + yl

    get_amp = pltpu.make_async_copy(amp.at[0], amp_v, in_sem.at[0])
    get_live = pltpu.make_async_copy(live_in, live, in_sem.at[1])
    get_rec = pltpu.make_async_copy(rec_in, rec, in_sem.at[2])
    get_neu = pltpu.make_async_copy(neu, nz.at[pl.ds(HERE, 1)], in_sem.at[3])
    my_rows = pl.ds(pl.multiple_of(me * 16, 16), 16)
    low_rows = pl.ds(pl.multiple_of(256 + me * 16, 16), 16)
    my_cols = pl.ds(pl.multiple_of(x * 512 + co * 256, 256), 256)
    own_l = pltpu.make_async_copy(lad.at[0, :, my_cols], wts.at[my_rows], w_r)
    own_c = pltpu.make_async_copy(cyc.at[0, :, my_cols], wts.at[low_rows], w_r)
    get_amp.start()
    get_live.start()

    def at_z(k):
        return (e, x * 32 + yl * 16 + lax.rem(z + k + 32, 16))

    def member(k):
        pe = rem(yh + 1 - div(k, 8), 2) * 2 + rem(co + 1 - rem(div(k, 4), 2), 2)
        px = rem(x + 3 - rem(k, 4), 4)
        return pe, px

    def near_z(k):
        return (4 - div(k, 2)) * (1 - 2 * rem(k, 2))

    bar = pltpu.get_barrier_semaphore()

    def greet(dev):
        pl.semaphore_signal(bar, inc=1, device_id=dev, device_id_type=MESH)

    for k in (1, 5, 0, 2, 4, 6, 9, 13):
        pe, px = member(k)
        greet((pe, px * 32 + yl * 16 + z))
        greet(at_z(near_z((1, 5, 0, 2, 4, 6, 9, 13).index(k))))
    for k in (3, 7, 8, 10, 11, 12, 14):
        pe, px = member(k)
        greet((pe, px * 32 + yl * 16 + z))

    def apart(p, q):
        ahead = lax.rem(p - q + 16, 16)
        return jnp.minimum(ahead, 16 - ahead)

    @pl.when(z < EARLY)
    def _():
        @pl.loop(LATE, 16)
        def _(s):
            @pl.when(apart(s, z) > 4)
            def _():
                greet((e, x * 32 + yl * 16 + s))

    for k in range(4):
        greet((k, x * 32 + (1 - yl) * 16 + z))
    for k in range(1, 4):
        greet((e, lax.rem(x + k, 4) * 32 + (1 - yl) * 16 + z))

    get_neu.start()
    get_rec.start()
    own_l.start()
    own_c.start()

    order = lanes_by_half()
    get_live.wait()
    alive = jnp.where(r < live[e], 1.0, 0.0).astype(F32)
    get_amp.wait()
    block = mm((amp_v[...].astype(F32) * alive).astype(BF16), order)
    zbuf[HERE * 16 : HERE * 16 + 16, :] = block.astype(BF16)

    straight = 0
    for d in range(EARLY):
        straight = straight + jnp.where(apart(z, d) > 4, 1, 0)
    pl.semaphore_wait(bar, 30 + jnp.where(z >= LATE, straight, 0))

    def send(src, dst, ss, rs, dev):
        return pltpu.make_async_remote_copy(
            src_ref=src, dst_ref=dst, send_sem=ss, recv_sem=rs,
            device_id=dev, device_id_type=MESH,
        )

    def z_rows(slot):
        return pl.ds(pl.multiple_of(slot * 16, 16), 16)

    def sender(k):
        return max(k - 7, 0) if isinstance(k, int) else k - 7

    def z_copy(k, slot, to):
        lands = rem(slot - to + 32, 16)
        return send(
            zbuf.at[z_rows(slot)], zbuf.at[z_rows(lands)], z_s.at[sender(k)],
            z_r.at[div(lands + 3, 4)], at_z(to)
        )

    def n_copy(k, slot, to):
        lands = rem(slot - to + 32, 16)
        return send(
            nz.at[pl.ds(slot, 1)], nz.at[pl.ds(lands, 1)], n_s.at[sender(k)],
            n_r.at[div(lands + 3, 4)], at_z(to)
        )

    def z_wait(first, last):
        here = zbuf.at[first * 16 : last * 16]
        send(here, here, z_s.at[0], z_r.at[(first + 3) // 4], at_z(1)).wait_recv()

    def n_wait(first, last):
        here = nz.at[first:last]
        send(here, here, n_s.at[0], n_r.at[(first + 3) // 4], at_z(1)).wait_recv()

    def goes_straight(source, to):
        return jnp.logical_and(
            lax.rem(z + source + 16, 16) >= LATE, lax.rem(z + to + 16, 16) < EARLY
        )

    def each_straight(act):
        @pl.when(z >= LATE)
        def _():
            @pl.loop(0, EARLY)
            def _(d):
                @pl.when(apart(z, d) > 4)
                def _():
                    act(15 + d, HERE, d - z)

    def each_low(act):
        @pl.loop(0, 4)
        def _(k):
            @pl.when(jnp.logical_not(goes_straight(-4, 4 - k)))
            def _():
                act(8 + k, 0, 4 - k)

    def each_high(act):
        @pl.loop(0, 3)
        def _(k):
            @pl.when(jnp.logical_not(goes_straight(4, k - 3)))
            def _():
                act(12 + k, 8, k - 3)

    def z_start(k, slot, to):
        z_copy(k, slot, to).start()

    def n_start(k, slot, to):
        n_copy(k, slot, to).start()

    def z_sent(k, slot, to):
        z_copy(k, slot, to).wait_send()

    def n_sent(k, slot, to):
        n_copy(k, slot, to).wait_send()

    each_straight(z_start)
    for k in range(8):
        z_copy(k, HERE, near_z(k)).start()

    def n1_copy(k):
        g = lax.rem(group + k, 8)
        rows = nall.at[pl.ds(pl.multiple_of(group * 32, 32), 32)]
        dev = (e, lax.div(g, 2) * 32 + lax.rem(g, 2) * 16 + z)
        return send(rows, rows, n1_s, n1_r, dev)

    my_e = pl.ds(pl.multiple_of(e * 16, 16), 16)

    def s_copy(k):
        rows = sall.at[my_e]
        return send(rows, rows, s_s, s_r, (lax.rem(e + k, 4), r))

    def w_copy(src, rows, k):
        pe, px = member(k)
        cols = pl.ds(pl.multiple_of(px * 512 + lax.rem(pe, 2) * 256, 256), 256)
        return send(
            src.at[0, :, cols], wts.at[rows], w_s, w_r, (pe, px * 32 + yl * 16 + z)
        )

    def all_here(ref, sem):
        send(ref, ref, sem, sem, at_z(1)).wait_recv()

    def all_gone(ref, sem):
        send(ref, ref, sem, sem, at_z(1)).wait_send()

    get_neu.wait()
    get_rec.wait()
    each_straight(n_start)
    for k in range(8):
        n_copy(k, HERE, near_z(k)).start()

    def weights_out():
        @pl.loop(0, 15)
        def _(k):
            w_copy(lad, my_rows, k).start()
            w_copy(cyc, low_rows, k).start()

    @pl.when(z < LATE)
    def _():
        weights_out()

    def away_y(k):
        y = lax.rem(yh * 2 + yl + lax.rem(k + 2, 4) + lax.div(k, 2) * (5 - 2 * k), 4)
        return lax.div(y, 2), lax.rem(y, 2)

    def part_rows(part):
        first, last = PARTS[part]
        return pl.ds(first * 16, (last - first) * 16)

    def a_copy(part, k):
        pyh, pyl = away_y(k)
        rows = part_rows(part)
        src = zbuf.at[rows, pl.ds(pl.multiple_of(pyh * 128, 128), 128)]
        dst = abuf.at[rows, pl.ds(pl.multiple_of(e * 128, 128), 128)]
        dev = (pyh * 2 + yl, x * 32 + pyl * 16 + z)
        return src, dst, a_s, a_r.at[part], dev

    def is_self(k):
        return jnp.logical_and(co == yl, k == 3)

    def a_start(part):
        @pl.loop(0, 4)
        def _(k):
            src, dst, ss, rs, dev = a_copy(part, k)
            own = is_self(k)

            @pl.when(own)
            def _():
                pltpu.make_async_copy(src, dst, rs).start()

            @pl.when(jnp.logical_not(own))
            def _():
                send(src, dst, ss, rs, dev).start()

    def a_sent():
        @pl.when(co == yl)
        def _():
            all_gone(abuf.at[:, 0:384], a_s)

        @pl.when(co != yl)
        def _():
            all_gone(abuf, a_s)

    def a_wait(part):
        all_here(abuf.at[part_rows(part)], a_r.at[part])

    z_wait(5, 9)
    each_high(z_start)
    a_start(0)
    z_wait(0, 1)
    each_low(z_start)
    z_wait(1, 4)
    a_start(1)
    n_wait(0, 1)
    each_low(n_start)
    n_wait(5, 9)
    each_high(n_start)

    @pl.when(z >= LATE)
    def _():
        weights_out()

    sall[my_e, :] = swap_rows_lanes(block).astype(BF16)

    @pl.loop(1, 4)
    def _(k):
        s_copy(k).start()

    def settle(first, last):
        value = abuf[first * 16 : last * 16, :]
        swapped = swap_rows_lanes(value.astype(F32)).astype(BF16)
        for slot in range(first, last):
            rows = pl.ds(pl.multiple_of(lax.rem(z + slot + 12, 16) * 16, 16), 16)
            at = (slot - first) * 16
            plain[rows, :] = value[at : at + 16]
            turned[rows, :] = swapped[at : at + 16]

    orders[0] = order
    orders[1] = lanes_back()
    orders[2] = neutron_row_order()

    all_here(wts, w_r)

    all_gone(sall.at[0:48], s_s)
    all_gone(wts.at[0:480], w_s)

    all_gone(zbuf.at[0:128], z_s.at[0])
    all_gone(nz.at[0:8], n_s.at[0])

    for part in (2, 3):
        z_wait(*PARTS[part])
        a_start(part)

    a_wait(0)
    a_wait(1)
    settle(0, 9)

    n_wait(1, 4)
    n_wait(9, 13)
    n_wait(13, 16)

    place = lax.broadcasted_iota(jnp.int32, (32, 256), 0)
    stacked = jnp.zeros((32, 256), F32)
    for slot in range(SLOTS):
        at = 2 * lax.rem(z + slot + 12, 16)
        pair = nz[slot].astype(F32)
        stacked = jnp.where(place == at, pair[0:1], stacked)
        stacked = jnp.where(place == at + 1, pair[1:2], stacked)
    nall[pl.ds(pl.multiple_of(group * 32, 32), 32), :] = stacked.astype(BF16)

    @pl.loop(1, 8)
    def _(k):
        n1_copy(k).start()

    for sent in (z_sent, n_sent):
        each_straight(sent)
        each_low(sent)
        each_high(sent)

    a_wait(2)
    settle(9, 13)
    a_wait(3)

    settle(13, 16)
    products = mm(wts[256:512, :], turned[...])
    for c in range(4):
        rows = slice(64 * c, 64 * c + 64)
        mixed = rec[c, 0] * products[rows, 0:128]
        for d in range(1, 4):
            mixed = mixed + rec[c, d] * products[rows, 128 * d : 128 * d + 128]
        fsend[rows, :] = swap_rows_lanes(mixed) + mm(
            wts[rows, :], plain[:, 128 * c : 128 * c + 128]
        )

    def f_copy(k):
        pe, px = member(k)
        rows = pl.ds(pl.multiple_of((pe * 4 + px) * 16, 16), 16)
        return send(
            fsend.at[rows], frecv.at[me], f_s, f_r,
            (pe, px * 32 + yl * 16 + z),
        )

    for k in (1, 5, 0, 2, 4, 6, 9, 13, 3, 7, 8, 10, 11, 12, 14):
        f_copy(k).start()

    frecv[me] = fsend[my_rows, :]

    all_here(sall.at[0:48], s_r)
    all_here(nall.at[0:224], n1_r)

    ordered = mm(orders[2], nall[...]).astype(BF16)
    ordered = mm(ordered, orders[0]).astype(BF16)
    terms = lax.dot_general(
        sall[...], ordered, (((1,), (1,)), ((), ())), preferred_element_type=F32
    )
    neutron = rec[e, 0] * terms[0:16]
    for c in range(1, 4):
        neutron = neutron + rec[e, c] * terms[16 * c : 16 * c + 16]
    neutron = swap_rows_lanes(neutron)

    a_sent()

    all_gone(nall.at[0:224], n1_s)
    all_gone(fsend.at[0:240], f_s)

    all_here(frecv.at[0:15], f_r)

    halves = []
    for h in range(2):
        total = neutron[:, 128 * h : 128 * h + 128]
        for s in range(2):
            for i in range(4):
                total = total + frecv[(2 * h + s) * 4 + i]
        halves.append((total * alive).astype(BF16))
    out[0] = mm(jnp.concatenate(halves, axis=1), orders[1]).astype(BF16)


def local(amplitudes, ladder_pp, cycle_proton, cycle_neutron, recouple, proton_live):
    dma = pltpu.SemaphoreType.DMA
    operands = (amplitudes, ladder_pp, cycle_proton, cycle_neutron, recouple, proton_live)
    return pl.pallas_call(
        kernel,
        out_shape=pltpu.VMEM((1, 16, 256), BF16),
        in_specs=[pl.BlockSpec(memory_space=pltpu.HBM)] * 6,
        out_specs=pl.BlockSpec(memory_space=pltpu.VMEM),
        scratch_shapes=[
            pltpu.SMEM((4, 4), F32),
            pltpu.SMEM((4,), jnp.int32),
            pltpu.VMEM((16, 256), BF16),
            pltpu.VMEM((256, 256), BF16),
            pltpu.VMEM((16, 2, 256), BF16),
            pltpu.VMEM((64, 256), BF16),
            pltpu.VMEM((256, 256), BF16),
            pltpu.VMEM((512, 256), BF16),
            pltpu.VMEM((256, 512), BF16),
            pltpu.VMEM((256, 512), BF16),
            pltpu.VMEM((256, 512), BF16),
            pltpu.VMEM((3, 256, 256), BF16),
            pltpu.VMEM((256, 128), F32),
            pltpu.VMEM((16, 16, 128), F32),
            dma((4,)),
            dma((8 + EARLY,)),
            dma((5,)),
            dma((8 + EARLY,)),
            dma((5,)),
            dma,
            dma,
            dma,
            dma,
            dma,
            dma,
            dma,
            dma((4,)),
            dma,
            dma,
        ],
        compiler_params=pltpu.CompilerParams(
            collective_id=0, has_side_effects=True, vmem_limit_bytes=16 << 20
        ),
        name="pair_residual",
    )(*(pltpu.with_memory_space_constraint(v, pltpu.HBM) for v in operands))


def solution(mesh):
    rows = P("chan", "row", None)
    return jax.shard_map(
        local,
        mesh=mesh,
        in_specs=(rows, rows, rows, rows, P(), P()),
        out_specs=rows,
        check_vma=False,
    )
```

```python
import jax
import jax.numpy as jnp
from jax import lax
from jax.experimental import pallas as pl
from jax.experimental.pallas import tpu as pltpu
from jax.sharding import PartitionSpec as P

MESH = pl.DeviceIdType.MESH
F32 = jnp.float32
BF16 = jnp.bfloat16


def swap_rows_lanes(v):
    n, width = v.shape
    lane = lax.broadcasted_iota(jnp.int32, (1, 1, width), 2)
    row = lax.broadcasted_iota(jnp.int32, (1, 8, 1), 1)
    v = v.reshape(n // 8, 8, width)
    for s in range(3):
        step, reach = 1 << s, 8 << s
        lane_bit = (lane & reach) != 0
        row_bit = (row & step) != 0
        down = pltpu.roll(pltpu.roll(v, width - reach, 2), step, 1)
        up = pltpu.roll(pltpu.roll(v, reach, 2), 8 - step, 1)
        moved = jnp.where(row_bit, down, up)
        v = jnp.where(jnp.logical_xor(lane_bit, row_bit), moved, v)
    lane_bit = (lane & 64) != 0
    v = v.reshape(n // 16, 2, 8, width)
    low, high = v[:, 0], v[:, 1]
    new_low = jnp.where(lane_bit, pltpu.roll(high, 64, 2), low)
    new_high = jnp.where(lane_bit, high, pltpu.roll(low, width - 64, 2))
    return jnp.stack([new_low, new_high], axis=1).reshape(n, width)


def lanes_by_half():
    old = lax.broadcasted_iota(jnp.int32, (256, 256), 0)
    new = lax.broadcasted_iota(jnp.int32, (256, 256), 1)
    goes = ((old >> 3) & 1) * 128 + (old >> 4) * 8 + (old & 7)
    return jnp.where(goes == new, 1.0, 0.0).astype(BF16)


def lanes_back():
    new = lax.broadcasted_iota(jnp.int32, (256, 256), 0)
    old = lax.broadcasted_iota(jnp.int32, (256, 256), 1)
    goes = ((old >> 3) & 1) * 128 + (old >> 4) * 8 + (old & 7)
    return jnp.where(goes == new, 1.0, 0.0).astype(BF16)


def neutron_row_order():
    new = lax.broadcasted_iota(jnp.int32, (256, 256), 0)
    old = lax.broadcasted_iota(jnp.int32, (256, 256), 1)
    z, t = (old >> 1) & 15, old & 1
    b = (old >> 5) * 2 + (z >> 3)
    goes = ((z >> 2) & 1) * 128 + b * 8 + (z & 3) * 2 + t
    return jnp.where(goes == new, 1.0, 0.0).astype(BF16)


def div(a, b):
    return a // b if isinstance(a, int) else lax.div(a, b)


def rem(a, b):
    return a % b if isinstance(a, int) else lax.rem(a, b)


def mm(a, b):
    return jnp.dot(a, b, preferred_element_type=F32)


SLOTS = 16
PARTS = ((4, 9), (0, 4), (9, 13), (13, 16))
LATE, EARLY = 8, 2
HERE = 4


def kernel(
    amp, lad, cyc, neu, rec_in, live_in, out,
    rec, live, amp_v, zbuf, nz, sall, nall, wts, abuf, plain, turned, orders, fsend, frecv,
    in_sem, z_s, z_r, n_s, n_r, s_s, s_r, n1_s, n1_r,
    w_s, w_r, a_s, a_r, f_s, f_r,
):
    e, r = lax.axis_index("chan"), lax.axis_index("row")
    yh, co = lax.div(e, 2), lax.rem(e, 2)
    x, yl, z = lax.div(r, 32), lax.rem(lax.div(r, 16), 2), lax.rem(r, 16)
    me = e * 4 + x
    group = x * 2 + yl

    get_amp = pltpu.make_async_copy(amp.at[0], amp_v, in_sem.at[0])
    get_live = pltpu.make_async_copy(live_in, live, in_sem.at[1])
    get_rec = pltpu.make_async_copy(rec_in, rec, in_sem.at[2])
    get_neu = pltpu.make_async_copy(neu, nz.at[pl.ds(HERE, 1)], in_sem.at[3])
    my_rows = pl.ds(pl.multiple_of(me * 16, 16), 16)
    low_rows = pl.ds(pl.multiple_of(256 + me * 16, 16), 16)
    my_cols = pl.ds(pl.multiple_of(x * 512 + co * 256, 256), 256)
    own_l = pltpu.make_async_copy(lad.at[0, :, my_cols], wts.at[my_rows], w_r)
    own_c = pltpu.make_async_copy(cyc.at[0, :, my_cols], wts.at[low_rows], w_r)
    get_amp.start()
    get_live.start()

    def at_z(k):
        return (e, x * 32 + yl * 16 + lax.rem(z + k + 32, 16))

    def member(k):
        pe = rem(yh + 1 - div(k, 8), 2) * 2 + rem(co + 1 - rem(div(k, 4), 2), 2)
        px = rem(x + 3 - rem(k, 4), 4)
        return pe, px

    def near_z(k):
        return (4 - div(k, 2)) * (1 - 2 * rem(k, 2))

    bar = pltpu.get_barrier_semaphore()

    def greet(dev):
        pl.semaphore_signal(bar, inc=1, device_id=dev, device_id_type=MESH)

    for k in (1, 5, 0, 2, 4, 6, 9, 13):
        pe, px = member(k)
        greet((pe, px * 32 + yl * 16 + z))
        greet(at_z(near_z((1, 5, 0, 2, 4, 6, 9, 13).index(k))))
    for k in (3, 7, 8, 10, 11, 12, 14):
        pe, px = member(k)
        greet((pe, px * 32 + yl * 16 + z))

    def apart(p, q):
        ahead = lax.rem(p - q + 16, 16)
        return jnp.minimum(ahead, 16 - ahead)

    @pl.when(z < EARLY)
    def _():
        @pl.loop(LATE, 16)
        def _(s):
            @pl.when(apart(s, z) > 4)
            def _():
                greet((e, x * 32 + yl * 16 + s))

    for k in range(4):
        greet((k, x * 32 + (1 - yl) * 16 + z))
    for k in range(1, 4):
        greet((e, lax.rem(x + k, 4) * 32 + (1 - yl) * 16 + z))

    get_neu.start()
    get_rec.start()
    own_l.start()
    own_c.start()

    order = lanes_by_half()
    get_live.wait()
    alive = jnp.where(r < live[e], 1.0, 0.0).astype(F32)
    get_amp.wait()
    block = mm((amp_v[...].astype(F32) * alive).astype(BF16), order)
    zbuf[HERE * 16 : HERE * 16 + 16, :] = block.astype(BF16)

    straight = 0
    for d in range(EARLY):
        straight = straight + jnp.where(apart(z, d) > 4, 1, 0)
    pl.semaphore_wait(bar, 30 + jnp.where(z >= LATE, straight, 0))

    def send(src, dst, ss, rs, dev):
        return pltpu.make_async_remote_copy(
            src_ref=src, dst_ref=dst, send_sem=ss, recv_sem=rs,
            device_id=dev, device_id_type=MESH,
        )

    def z_rows(slot):
        return pl.ds(pl.multiple_of(slot * 16, 16), 16)

    def sender(k):
        return max(k - 7, 0) if isinstance(k, int) else k - 7

    def z_copy(k, slot, to):
        lands = rem(slot - to + 32, 16)
        return send(
            zbuf.at[z_rows(slot)], zbuf.at[z_rows(lands)], z_s.at[sender(k)],
            z_r.at[div(lands + 3, 4)], at_z(to)
        )

    def n_copy(k, slot, to):
        lands = rem(slot - to + 32, 16)
        return send(
            nz.at[pl.ds(slot, 1)], nz.at[pl.ds(lands, 1)], n_s.at[sender(k)],
            n_r.at[div(lands + 3, 4)], at_z(to)
        )

    def z_wait(first, last):
        here = zbuf.at[first * 16 : last * 16]
        send(here, here, z_s.at[0], z_r.at[(first + 3) // 4], at_z(1)).wait_recv()

    def n_wait(first, last):
        here = nz.at[first:last]
        send(here, here, n_s.at[0], n_r.at[(first + 3) // 4], at_z(1)).wait_recv()

    def goes_straight(source, to):
        return jnp.logical_and(
            lax.rem(z + source + 16, 16) >= LATE, lax.rem(z + to + 16, 16) < EARLY
        )

    def each_straight(act):
        @pl.when(z >= LATE)
        def _():
            @pl.loop(0, EARLY)
            def _(d):
                @pl.when(apart(z, d) > 4)
                def _():
                    act(15 + d, HERE, d - z)

    def each_low(act):
        @pl.loop(0, 4)
        def _(k):
            @pl.when(jnp.logical_not(goes_straight(-4, 4 - k)))
            def _():
                act(8 + k, 0, 4 - k)

    def each_high(act):
        @pl.loop(0, 3)
        def _(k):
            @pl.when(jnp.logical_not(goes_straight(4, k - 3)))
            def _():
                act(12 + k, 8, k - 3)

    def z_start(k, slot, to):
        z_copy(k, slot, to).start()

    def n_start(k, slot, to):
        n_copy(k, slot, to).start()

    def z_sent(k, slot, to):
        z_copy(k, slot, to).wait_send()

    def n_sent(k, slot, to):
        n_copy(k, slot, to).wait_send()

    each_straight(z_start)
    for k in range(8):
        z_copy(k, HERE, near_z(k)).start()

    def n1_copy(k):
        g = lax.rem(group + k, 8)
        rows = nall.at[pl.ds(pl.multiple_of(group * 32, 32), 32)]
        dev = (e, lax.div(g, 2) * 32 + lax.rem(g, 2) * 16 + z)
        return send(rows, rows, n1_s, n1_r, dev)

    my_e = pl.ds(pl.multiple_of(e * 16, 16), 16)

    def s_copy(k):
        rows = sall.at[my_e]
        return send(rows, rows, s_s, s_r, (lax.rem(e + k, 4), r))

    def w_copy(src, rows, k):
        pe, px = member(k)
        cols = pl.ds(pl.multiple_of(px * 512 + lax.rem(pe, 2) * 256, 256), 256)
        return send(
            src.at[0, :, cols], wts.at[rows], w_s, w_r, (pe, px * 32 + yl * 16 + z)
        )

    def all_here(ref, sem):
        send(ref, ref, sem, sem, at_z(1)).wait_recv()

    def all_gone(ref, sem):
        send(ref, ref, sem, sem, at_z(1)).wait_send()

    get_neu.wait()
    get_rec.wait()
    each_straight(n_start)
    for k in range(8):
        n_copy(k, HERE, near_z(k)).start()

    def weights_out():
        @pl.loop(0, 15)
        def _(k):
            w_copy(lad, my_rows, k).start()
            w_copy(cyc, low_rows, k).start()

    @pl.when(z < LATE)
    def _():
        weights_out()

    def away_y(k):
        y = lax.rem(yh * 2 + yl + lax.rem(k + 2, 4) + lax.div(k, 2) * (5 - 2 * k), 4)
        return lax.div(y, 2), lax.rem(y, 2)

    def part_rows(part):
        first, last = PARTS[part]
        return pl.ds(first * 16, (last - first) * 16)

    def a_copy(part, k):
        pyh, pyl = away_y(k)
        rows = part_rows(part)
        src = zbuf.at[rows, pl.ds(pl.multiple_of(pyh * 128, 128), 128)]
        dst = abuf.at[rows, pl.ds(pl.multiple_of(e * 128, 128), 128)]
        dev = (pyh * 2 + yl, x * 32 + pyl * 16 + z)
        return src, dst, a_s, a_r.at[part], dev

    def is_self(k):
        return jnp.logical_and(co == yl, k == 3)

    def a_start(part):
        @pl.loop(0, 4)
        def _(k):
            src, dst, ss, rs, dev = a_copy(part, k)
            own = is_self(k)

            @pl.when(own)
            def _():
                pltpu.make_async_copy(src, dst, rs).start()

            @pl.when(jnp.logical_not(own))
            def _():
                send(src, dst, ss, rs, dev).start()

    def a_sent():
        @pl.when(co == yl)
        def _():
            all_gone(abuf.at[:, 0:384], a_s)

        @pl.when(co != yl)
        def _():
            all_gone(abuf, a_s)

    def a_wait(part):
        all_here(abuf.at[part_rows(part)], a_r.at[part])

    z_wait(5, 9)
    each_high(z_start)
    z_wait(0, 1)
    each_low(z_start)
    a_start(0)
    z_wait(1, 4)
    a_start(1)
    n_wait(0, 1)
    each_low(n_start)
    n_wait(5, 9)
    each_high(n_start)

    @pl.when(z >= LATE)
    def _():
        weights_out()

    sall[my_e, :] = swap_rows_lanes(block).astype(BF16)

    @pl.loop(1, 4)
    def _(k):
        s_copy(k).start()

    def settle(first, last):
        value = abuf[first * 16 : last * 16, :]
        swapped = swap_rows_lanes(value.astype(F32)).astype(BF16)
        for slot in range(first, last):
            rows = pl.ds(pl.multiple_of(lax.rem(z + slot + 12, 16) * 16, 16), 16)
            at = (slot - first) * 16
            plain[rows, :] = value[at : at + 16]
            turned[rows, :] = swapped[at : at + 16]

    orders[0] = order
    orders[1] = lanes_back()
    orders[2] = neutron_row_order()

    all_here(wts, w_r)

    all_gone(sall.at[0:48], s_s)
    all_gone(wts.at[0:480], w_s)

    all_gone(zbuf.at[0:128], z_s.at[0])
    all_gone(nz.at[0:8], n_s.at[0])

    for part in (2, 3):
        z_wait(*PARTS[part])
        a_start(part)

    a_wait(0)
    a_wait(1)
    settle(0, 9)

    n_wait(1, 4)
    n_wait(9, 13)
    n_wait(13, 16)

    place = lax.broadcasted_iota(jnp.int32, (32, 256), 0)
    stacked = jnp.zeros((32, 256), F32)
    for slot in range(SLOTS):
        at = 2 * lax.rem(z + slot + 12, 16)
        pair = nz[slot].astype(F32)
        stacked = jnp.where(place == at, pair[0:1], stacked)
        stacked = jnp.where(place == at + 1, pair[1:2], stacked)
    nall[pl.ds(pl.multiple_of(group * 32, 32), 32), :] = stacked.astype(BF16)

    @pl.loop(1, 8)
    def _(k):
        n1_copy(k).start()

    for sent in (z_sent, n_sent):
        each_straight(sent)
        each_low(sent)
        each_high(sent)

    a_wait(2)
    settle(9, 13)
    a_wait(3)

    settle(13, 16)
    products = mm(wts[256:512, :], turned[...])
    for c in range(4):
        rows = slice(64 * c, 64 * c + 64)
        mixed = rec[c, 0] * products[rows, 0:128]
        for d in range(1, 4):
            mixed = mixed + rec[c, d] * products[rows, 128 * d : 128 * d + 128]
        fsend[rows, :] = swap_rows_lanes(mixed) + mm(
            wts[rows, :], plain[:, 128 * c : 128 * c + 128]
        )

    def f_copy(k):
        pe, px = member(k)
        rows = pl.ds(pl.multiple_of((pe * 4 + px) * 16, 16), 16)
        return send(
            fsend.at[rows], frecv.at[me], f_s, f_r,
            (pe, px * 32 + yl * 16 + z),
        )

    for k in (1, 5, 0, 2, 4, 6, 9, 13, 3, 7, 8, 10, 11, 12, 14):
        f_copy(k).start()

    frecv[me] = fsend[my_rows, :]

    all_here(sall.at[0:48], s_r)
    all_here(nall.at[0:224], n1_r)

    ordered = mm(orders[2], nall[...]).astype(BF16)
    ordered = mm(ordered, orders[0]).astype(BF16)
    terms = lax.dot_general(
        sall[...], ordered, (((1,), (1,)), ((), ())), preferred_element_type=F32
    )
    neutron = rec[e, 0] * terms[0:16]
    for c in range(1, 4):
        neutron = neutron + rec[e, c] * terms[16 * c : 16 * c + 16]
    neutron = swap_rows_lanes(neutron)

    a_sent()

    all_gone(nall.at[0:224], n1_s)
    all_gone(fsend.at[0:240], f_s)

    all_here(frecv.at[0:15], f_r)

    halves = []
    for h in range(2):
        total = neutron[:, 128 * h : 128 * h + 128]
        for s in range(2):
            for i in range(4):
                total = total + frecv[(2 * h + s) * 4 + i]
        halves.append((total * alive).astype(BF16))
    out[0] = mm(jnp.concatenate(halves, axis=1), orders[1]).astype(BF16)


def local(amplitudes, ladder_pp, cycle_proton, cycle_neutron, recouple, proton_live):
    dma = pltpu.SemaphoreType.DMA
    operands = (amplitudes, ladder_pp, cycle_proton, cycle_neutron, recouple, proton_live)
    return pl.pallas_call(
        kernel,
        out_shape=pltpu.VMEM((1, 16, 256), BF16),
        in_specs=[pl.BlockSpec(memory_space=pltpu.HBM)] * 6,
        out_specs=pl.BlockSpec(memory_space=pltpu.VMEM),
        scratch_shapes=[
            pltpu.SMEM((4, 4), F32),
            pltpu.SMEM((4,), jnp.int32),
            pltpu.VMEM((16, 256), BF16),
            pltpu.VMEM((256, 256), BF16),
            pltpu.VMEM((16, 2, 256), BF16),
            pltpu.VMEM((64, 256), BF16),
            pltpu.VMEM((256, 256), BF16),
            pltpu.VMEM((512, 256), BF16),
            pltpu.VMEM((256, 512), BF16),
            pltpu.VMEM((256, 512), BF16),
            pltpu.VMEM((256, 512), BF16),
            pltpu.VMEM((3, 256, 256), BF16),
            pltpu.VMEM((256, 128), F32),
            pltpu.VMEM((16, 16, 128), F32),
            dma((4,)),
            dma((8 + EARLY,)),
            dma((5,)),
            dma((8 + EARLY,)),
            dma((5,)),
            dma,
            dma,
            dma,
            dma,
            dma,
            dma,
            dma,
            dma((4,)),
            dma,
            dma,
        ],
        compiler_params=pltpu.CompilerParams(
            collective_id=0, has_side_effects=True, vmem_limit_bytes=16 << 20
        ),
        name="pair_residual",
    )(*(pltpu.with_memory_space_constraint(v, pltpu.HBM) for v in operands))


def solution(mesh):
    rows = P("chan", "row", None)
    return jax.shard_map(
        local,
        mesh=mesh,
        in_specs=(rows, rows, rows, rows, P(), P()),
        out_specs=rows,
        check_vma=False,
    )
```

```python
import jax
import jax.numpy as jnp
from jax import lax
from jax.experimental import pallas as pl
from jax.experimental.pallas import tpu as pltpu
from jax.sharding import PartitionSpec as P

MESH = pl.DeviceIdType.MESH
F32 = jnp.float32
BF16 = jnp.bfloat16


def swap_rows_lanes(v):
    n, width = v.shape
    lane = lax.broadcasted_iota(jnp.int32, (1, 1, width), 2)
    row = lax.broadcasted_iota(jnp.int32, (1, 8, 1), 1)
    v = v.reshape(n // 8, 8, width)
    for s in range(3):
        step, reach = 1 << s, 8 << s
        lane_bit = (lane & reach) != 0
        row_bit = (row & step) != 0
        down = pltpu.roll(pltpu.roll(v, width - reach, 2), step, 1)
        up = pltpu.roll(pltpu.roll(v, reach, 2), 8 - step, 1)
        moved = jnp.where(row_bit, down, up)
        v = jnp.where(jnp.logical_xor(lane_bit, row_bit), moved, v)
    lane_bit = (lane & 64) != 0
    v = v.reshape(n // 16, 2, 8, width)
    low, high = v[:, 0], v[:, 1]
    new_low = jnp.where(lane_bit, pltpu.roll(high, 64, 2), low)
    new_high = jnp.where(lane_bit, high, pltpu.roll(low, width - 64, 2))
    return jnp.stack([new_low, new_high], axis=1).reshape(n, width)


def lanes_by_half():
    old = lax.broadcasted_iota(jnp.int32, (256, 256), 0)
    new = lax.broadcasted_iota(jnp.int32, (256, 256), 1)
    goes = ((old >> 3) & 1) * 128 + (old >> 4) * 8 + (old & 7)
    return jnp.where(goes == new, 1.0, 0.0).astype(BF16)


def lanes_back():
    new = lax.broadcasted_iota(jnp.int32, (256, 256), 0)
    old = lax.broadcasted_iota(jnp.int32, (256, 256), 1)
    goes = ((old >> 3) & 1) * 128 + (old >> 4) * 8 + (old & 7)
    return jnp.where(goes == new, 1.0, 0.0).astype(BF16)


def neutron_row_order():
    new = lax.broadcasted_iota(jnp.int32, (256, 256), 0)
    old = lax.broadcasted_iota(jnp.int32, (256, 256), 1)
    z, t = (old >> 1) & 15, old & 1
    b = (old >> 5) * 2 + (z >> 3)
    goes = ((z >> 2) & 1) * 128 + b * 8 + (z & 3) * 2 + t
    return jnp.where(goes == new, 1.0, 0.0).astype(BF16)


def div(a, b):
    return a // b if isinstance(a, int) else lax.div(a, b)


def rem(a, b):
    return a % b if isinstance(a, int) else lax.rem(a, b)


def mm(a, b):
    return jnp.dot(a, b, preferred_element_type=F32)


SLOTS = 16
PARTS = ((4, 9), (0, 4), (9, 13), (13, 16))
LATE, EARLY = 8, 2
HERE = 4


def kernel(
    amp, lad, cyc, neu, rec_in, live_in, out,
    rec, live, amp_v, zbuf, nz, sall, nall, wts, abuf, plain, turned, orders, fsend, frecv,
    in_sem, z_s, z_r, n_s, n_r, s_s, s_r, n1_s, n1_r,
    w_s, w_r, a_s, a_r, f_s, f_r,
):
    e, r = lax.axis_index("chan"), lax.axis_index("row")
    yh, co = lax.div(e, 2), lax.rem(e, 2)
    x, yl, z = lax.div(r, 32), lax.rem(lax.div(r, 16), 2), lax.rem(r, 16)
    me = e * 4 + x
    group = x * 2 + yl

    get_amp = pltpu.make_async_copy(amp.at[0], amp_v, in_sem.at[0])
    get_live = pltpu.make_async_copy(live_in, live, in_sem.at[1])
    get_rec = pltpu.make_async_copy(rec_in, rec, in_sem.at[2])
    get_neu = pltpu.make_async_copy(neu, nz.at[pl.ds(HERE, 1)], in_sem.at[3])
    my_rows = pl.ds(pl.multiple_of(me * 16, 16), 16)
    low_rows = pl.ds(pl.multiple_of(256 + me * 16, 16), 16)
    my_cols = pl.ds(pl.multiple_of(x * 512 + co * 256, 256), 256)
    own_l = pltpu.make_async_copy(lad.at[0, :, my_cols], wts.at[my_rows], w_r)
    own_c = pltpu.make_async_copy(cyc.at[0, :, my_cols], wts.at[low_rows], w_r)

    def at_z(k):
        return (e, x * 32 + yl * 16 + lax.rem(z + k + 32, 16))

    def member(k):
        pe = rem(yh + 1 - div(k, 8), 2) * 2 + rem(co + 1 - rem(div(k, 4), 2), 2)
        px = rem(x + 3 - rem(k, 4), 4)
        return pe, px

    def near_z(k):
        return (4 - div(k, 2)) * (1 - 2 * rem(k, 2))

    bar = pltpu.get_barrier_semaphore()

    def greet(dev):
        pl.semaphore_signal(bar, inc=1, device_id=dev, device_id_type=MESH)

    for k in (1, 5, 0, 2, 4, 6, 9, 13):
        pe, px = member(k)
        greet((pe, px * 32 + yl * 16 + z))
        greet(at_z(near_z((1, 5, 0, 2, 4, 6, 9, 13).index(k))))
    get_amp.start()
    get_live.start()
    for k in (3, 7, 8, 10, 11, 12, 14):
        pe, px = member(k)
        greet((pe, px * 32 + yl * 16 + z))

    def apart(p, q):
        ahead = lax.rem(p - q + 16, 16)
        return jnp.minimum(ahead, 16 - ahead)

    @pl.when(z < EARLY)
    def _():
        @pl.loop(LATE, 16)
        def _(s):
            @pl.when(apart(s, z) > 4)
            def _():
                greet((e, x * 32 + yl * 16 + s))

    for k in range(4):
        greet((k, x * 32 + (1 - yl) * 16 + z))
    for k in range(1, 4):
        greet((e, lax.rem(x + k, 4) * 32 + (1 - yl) * 16 + z))

    get_neu.start()
    get_rec.start()
    own_l.start()
    own_c.start()

    order = lanes_by_half()
    get_live.wait()
    alive = jnp.where(r < live[e], 1.0, 0.0).astype(F32)
    get_amp.wait()
    block = mm((amp_v[...].astype(F32) * alive).astype(BF16), order)
    zbuf[HERE * 16 : HERE * 16 + 16, :] = block.astype(BF16)

    straight = 0
    for d in range(EARLY):
        straight = straight + jnp.where(apart(z, d) > 4, 1, 0)
    pl.semaphore_wait(bar, 30 + jnp.where(z >= LATE, straight, 0))

    def send(src, dst, ss, rs, dev):
        return pltpu.make_async_remote_copy(
            src_ref=src, dst_ref=dst, send_sem=ss, recv_sem=rs,
            device_id=dev, device_id_type=MESH,
        )

    def z_rows(slot):
        return pl.ds(pl.multiple_of(slot * 16, 16), 16)

    def sender(k):
        return max(k - 7, 0) if isinstance(k, int) else k - 7

    def z_copy(k, slot, to):
        lands = rem(slot - to + 32, 16)
        return send(
            zbuf.at[z_rows(slot)], zbuf.at[z_rows(lands)], z_s.at[sender(k)],
            z_r.at[div(lands + 3, 4)], at_z(to)
        )

    def n_copy(k, slot, to):
        lands = rem(slot - to + 32, 16)
        return send(
            nz.at[pl.ds(slot, 1)], nz.at[pl.ds(lands, 1)], n_s.at[sender(k)],
            n_r.at[div(lands + 3, 4)], at_z(to)
        )

    def z_wait(first, last):
        here = zbuf.at[first * 16 : last * 16]
        send(here, here, z_s.at[0], z_r.at[(first + 3) // 4], at_z(1)).wait_recv()

    def n_wait(first, last):
        here = nz.at[first:last]
        send(here, here, n_s.at[0], n_r.at[(first + 3) // 4], at_z(1)).wait_recv()

    def goes_straight(source, to):
        return jnp.logical_and(
            lax.rem(z + source + 16, 16) >= LATE, lax.rem(z + to + 16, 16) < EARLY
        )

    def each_straight(act):
        @pl.when(z >= LATE)
        def _():
            @pl.loop(0, EARLY)
            def _(d):
                @pl.when(apart(z, d) > 4)
                def _():
                    act(15 + d, HERE, d - z)

    def each_low(act):
        @pl.loop(0, 4)
        def _(k):
            @pl.when(jnp.logical_not(goes_straight(-4, 4 - k)))
            def _():
                act(8 + k, 0, 4 - k)

    def each_high(act):
        @pl.loop(0, 3)
        def _(k):
            @pl.when(jnp.logical_not(goes_straight(4, k - 3)))
            def _():
                act(12 + k, 8, k - 3)

    def z_start(k, slot, to):
        z_copy(k, slot, to).start()

    def n_start(k, slot, to):
        n_copy(k, slot, to).start()

    def z_sent(k, slot, to):
        z_copy(k, slot, to).wait_send()

    def n_sent(k, slot, to):
        n_copy(k, slot, to).wait_send()

    each_straight(z_start)
    for k in range(8):
        z_copy(k, HERE, near_z(k)).start()

    def n1_copy(k):
        g = lax.rem(group + k, 8)
        rows = nall.at[pl.ds(pl.multiple_of(group * 32, 32), 32)]
        dev = (e, lax.div(g, 2) * 32 + lax.rem(g, 2) * 16 + z)
        return send(rows, rows, n1_s, n1_r, dev)

    my_e = pl.ds(pl.multiple_of(e * 16, 16), 16)

    def s_copy(k):
        rows = sall.at[my_e]
        return send(rows, rows, s_s, s_r, (lax.rem(e + k, 4), r))

    def w_copy(src, rows, k):
        pe, px = member(k)
        cols = pl.ds(pl.multiple_of(px * 512 + lax.rem(pe, 2) * 256, 256), 256)
        return send(
            src.at[0, :, cols], wts.at[rows], w_s, w_r, (pe, px * 32 + yl * 16 + z)
        )

    def all_here(ref, sem):
        send(ref, ref, sem, sem, at_z(1)).wait_recv()

    def all_gone(ref, sem):
        send(ref, ref, sem, sem, at_z(1)).wait_send()

    get_neu.wait()
    get_rec.wait()
    each_straight(n_start)
    for k in range(8):
        n_copy(k, HERE, near_z(k)).start()

    def weights_out():
        @pl.loop(0, 15)
        def _(k):
            w_copy(lad, my_rows, k).start()
            w_copy(cyc, low_rows, k).start()

    @pl.when(z < LATE)
    def _():
        weights_out()

    def away_y(k):
        y = lax.rem(yh * 2 + yl + lax.rem(k + 2, 4) + lax.div(k, 2) * (5 - 2 * k), 4)
        return lax.div(y, 2), lax.rem(y, 2)

    def part_rows(part):
        first, last = PARTS[part]
        return pl.ds(first * 16, (last - first) * 16)

    def a_copy(part, k):
        pyh, pyl = away_y(k)
        rows = part_rows(part)
        src = zbuf.at[rows, pl.ds(pl.multiple_of(pyh * 128, 128), 128)]
        dst = abuf.at[rows, pl.ds(pl.multiple_of(e * 128, 128), 128)]
        dev = (pyh * 2 + yl, x * 32 + pyl * 16 + z)
        return src, dst, a_s, a_r.at[part], dev

    def is_self(k):
        return jnp.logical_and(co == yl, k == 3)

    def a_start(part):
        @pl.loop(0, 4)
        def _(k):
            src, dst, ss, rs, dev = a_copy(part, k)
            own = is_self(k)

            @pl.when(own)
            def _():
                pltpu.make_async_copy(src, dst, rs).start()

            @pl.when(jnp.logical_not(own))
            def _():
                send(src, dst, ss, rs, dev).start()

    def a_sent():
        @pl.when(co == yl)
        def _():
            all_gone(abuf.at[:, 0:384], a_s)

        @pl.when(co != yl)
        def _():
            all_gone(abuf, a_s)

    def a_wait(part):
        all_here(abuf.at[part_rows(part)], a_r.at[part])

    z_wait(5, 9)
    each_high(z_start)
    z_wait(0, 1)
    each_low(z_start)
    a_start(0)
    z_wait(1, 4)
    a_start(1)
    n_wait(0, 1)
    each_low(n_start)
    n_wait(5, 9)
    each_high(n_start)

    @pl.when(z >= LATE)
    def _():
        weights_out()

    sall[my_e, :] = swap_rows_lanes(block).astype(BF16)

    @pl.loop(1, 4)
    def _(k):
        s_copy(k).start()

    def settle(first, last):
        value = abuf[first * 16 : last * 16, :]
        swapped = swap_rows_lanes(value.astype(F32)).astype(BF16)
        for slot in range(first, last):
            rows = pl.ds(pl.multiple_of(lax.rem(z + slot + 12, 16) * 16, 16), 16)
            at = (slot - first) * 16
            plain[rows, :] = value[at : at + 16]
            turned[rows, :] = swapped[at : at + 16]

    orders[0] = order
    orders[1] = lanes_back()
    orders[2] = neutron_row_order()

    all_here(wts, w_r)

    all_gone(sall.at[0:48], s_s)
    all_gone(wts.at[0:480], w_s)

    all_gone(zbuf.at[0:128], z_s.at[0])
    all_gone(nz.at[0:8], n_s.at[0])

    for part in (2, 3):
        z_wait(*PARTS[part])
        a_start(part)

    a_wait(0)
    a_wait(1)
    settle(0, 9)

    n_wait(1, 4)
    n_wait(9, 13)
    n_wait(13, 16)

    place = lax.broadcasted_iota(jnp.int32, (32, 256), 0)
    stacked = jnp.zeros((32, 256), F32)
    for slot in range(SLOTS):
        at = 2 * lax.rem(z + slot + 12, 16)
        pair = nz[slot].astype(F32)
        stacked = jnp.where(place == at, pair[0:1], stacked)
        stacked = jnp.where(place == at + 1, pair[1:2], stacked)
    nall[pl.ds(pl.multiple_of(group * 32, 32), 32), :] = stacked.astype(BF16)

    @pl.loop(1, 8)
    def _(k):
        n1_copy(k).start()

    for sent in (z_sent, n_sent):
        each_straight(sent)
        each_low(sent)
        each_high(sent)

    a_wait(2)
    settle(9, 13)
    a_wait(3)

    settle(13, 16)
    products = mm(wts[256:512, :], turned[...])
    for c in range(4):
        rows = slice(64 * c, 64 * c + 64)
        mixed = rec[c, 0] * products[rows, 0:128]
        for d in range(1, 4):
            mixed = mixed + rec[c, d] * products[rows, 128 * d : 128 * d + 128]
        fsend[rows, :] = swap_rows_lanes(mixed) + mm(
            wts[rows, :], plain[:, 128 * c : 128 * c + 128]
        )

    def f_copy(k):
        pe, px = member(k)
        rows = pl.ds(pl.multiple_of((pe * 4 + px) * 16, 16), 16)
        return send(
            fsend.at[rows], frecv.at[me], f_s, f_r,
            (pe, px * 32 + yl * 16 + z),
        )

    for k in (1, 5, 0, 2, 4, 6, 9, 13, 3, 7, 8, 10, 11, 12, 14):
        f_copy(k).start()

    frecv[me] = fsend[my_rows, :]

    all_here(sall.at[0:48], s_r)
    all_here(nall.at[0:224], n1_r)

    ordered = mm(orders[2], nall[...]).astype(BF16)
    ordered = mm(ordered, orders[0]).astype(BF16)
    terms = lax.dot_general(
        sall[...], ordered, (((1,), (1,)), ((), ())), preferred_element_type=F32
    )
    neutron = rec[e, 0] * terms[0:16]
    for c in range(1, 4):
        neutron = neutron + rec[e, c] * terms[16 * c : 16 * c + 16]
    neutron = swap_rows_lanes(neutron)

    a_sent()

    all_gone(nall.at[0:224], n1_s)
    all_gone(fsend.at[0:240], f_s)

    all_here(frecv.at[0:15], f_r)

    halves = []
    for h in range(2):
        total = neutron[:, 128 * h : 128 * h + 128]
        for s in range(2):
            for i in range(4):
                total = total + frecv[(2 * h + s) * 4 + i]
        halves.append((total * alive).astype(BF16))
    out[0] = mm(jnp.concatenate(halves, axis=1), orders[1]).astype(BF16)


def local(amplitudes, ladder_pp, cycle_proton, cycle_neutron, recouple, proton_live):
    dma = pltpu.SemaphoreType.DMA
    operands = (amplitudes, ladder_pp, cycle_proton, cycle_neutron, recouple, proton_live)
    return pl.pallas_call(
        kernel,
        out_shape=pltpu.VMEM((1, 16, 256), BF16),
        in_specs=[pl.BlockSpec(memory_space=pltpu.HBM)] * 6,
        out_specs=pl.BlockSpec(memory_space=pltpu.VMEM),
        scratch_shapes=[
            pltpu.SMEM((4, 4), F32),
            pltpu.SMEM((4,), jnp.int32),
            pltpu.VMEM((16, 256), BF16),
            pltpu.VMEM((256, 256), BF16),
            pltpu.VMEM((16, 2, 256), BF16),
            pltpu.VMEM((64, 256), BF16),
            pltpu.VMEM((256, 256), BF16),
            pltpu.VMEM((512, 256), BF16),
            pltpu.VMEM((256, 512), BF16),
            pltpu.VMEM((256, 512), BF16),
            pltpu.VMEM((256, 512), BF16),
            pltpu.VMEM((3, 256, 256), BF16),
            pltpu.VMEM((256, 128), F32),
            pltpu.VMEM((16, 16, 128), F32),
            dma((4,)),
            dma((8 + EARLY,)),
            dma((5,)),
            dma((8 + EARLY,)),
            dma((5,)),
            dma,
            dma,
            dma,
            dma,
            dma,
            dma,
            dma,
            dma((4,)),
            dma,
            dma,
        ],
        compiler_params=pltpu.CompilerParams(
            collective_id=0, has_side_effects=True, vmem_limit_bytes=16 << 20
        ),
        name="pair_residual",
    )(*(pltpu.with_memory_space_constraint(v, pltpu.HBM) for v in operands))


def solution(mesh):
    rows = P("chan", "row", None)
    return jax.shard_map(
        local,
        mesh=mesh,
        in_specs=(rows, rows, rows, rows, P(), P()),
        out_specs=rows,
        check_vma=False,
    )
```
